32 devices in a mesh: dp: 4 (over y, x), seq: 8 (over z, core).
Axes of the slice: x: 2, y: 2, z: 4, core: 2. Of those that a mesh axis runs over, the one named last changes fastest.
Arguments:
- layer_input: bfloat16 [4, 1024, 2048], P('dp', 'seq'), may hold values from -6 to 6
- segment_ids: int32 [4, 1024], P('dp'), may hold values from 0 to 7, never falling along the last dimension, each value on 1 to 512 neighbouring positions
- first_gain: bfloat16 [2048], P(('dp', 'seq')), may hold values from 0.5 to 1.5
- query_down: bfloat16 [2048, 1024], P(('dp', 'seq')), may hold values from -0.125 to 0.125
- query_gain: bfloat16 [1024], P(('dp', 'seq')), may hold values from 0.5 to 1.5
- query_up: bfloat16 [1024, 4096], P(('dp', 'seq')), may hold values from -0.1875 to 0.1875
- key_proj: bfloat16 [2048, 256], P(('dp', 'seq')), may hold values from -0.125 to 0.125
- value_proj: bfloat16 [2048, 256], P(('dp', 'seq')), may hold values from -0.125 to 0.125
- out_proj: bfloat16 [4096, 2048], P(('dp', 'seq')), may hold values from -0.75 to 0.75
- second_gain: bfloat16 [2048], P(('dp', 'seq')), may hold values from 0.5 to 1.5
- w_gate: bfloat16 [2048, 5632], P(None, 'seq'), may hold values from -0.125 to 0.125
- w_up: bfloat16 [2048, 5632], P(None, 'seq'), may hold values from -0.125 to 0.125
- w_down: bfloat16 [5632, 2048], P('seq'), may hold values from -0.078125 to 0.078125
- cotangent: bfloat16 [4, 1024, 2048], P('dp', 'seq'), may hold values from -6 to 6
Outputs:
- layer_out: float32 [4, 1024, 2048], P('dp', 'seq')
- d_input: float32 [4, 1024, 2048], P('dp', 'seq')
- d_first: float32 [2048], P(('dp', 'seq'))
- d_qdown: float32 [2048, 1024], P(('dp', 'seq'))
- d_qgain: float32 [1024], P(('dp', 'seq'))
- d_qup: float32 [1024, 4096], P(('dp', 'seq'))
- d_key: float32 [2048, 256], P(('dp', 'seq'))
- d_value: float32 [2048, 256], P(('dp', 'seq'))
- d_out: float32 [4096, 2048], P(('dp', 'seq'))
- d_second: float32 [2048], P(('dp', 'seq'))
- d_gate: float32 [2048, 5632], P(None, 'seq')
- d_up: float32 [2048, 5632], P(None, 'seq')
- d_down: float32 [5632, 2048], P('seq')
The draws below stay inside these ranges and needn't reach their ends.
Inputs may be any that keep to these rules, and one draw needn't show every extreme that they name: `segment_ids`: along a row the numbers never fall; every number of a row holds 1 to 512 consecutive tokens, and one holds exactly 512.
All inputs are finite; a program needn't handle non-finite values.
Results may differ from the reference program's by a relative error of at most 0.015.
Values may be sent and summed in bfloat16 or wider, within the bound.
No kernel may reach another device: no remote copies, remote signals or barrier semaphores. Data moves between devices by JAX's collectives and lax.ppermute only.
A program may use at most 384 MiB of HBM per device.

```python
import math
import jax
import jax.numpy as jnp
import numpy as np
from jax import lax

D = 2048
DQ = 1024
HEADS = 16
HEAD = 256
FF = 5632
SEGS = 8
LEN = 1024
ROWS = 4


def level_of(rng, dims, split, low, top_value):
    factor_of, own = 1.0, jax.random.fold_in(rng, 6)
    for axis_at, shards_of in split:
        draws = jnp.exp(jax.random.uniform(jax.random.fold_in(own, axis_at), (shards_of,), jnp.float32, low / len(split), top_value / len(split)))
        factor_of = factor_of * jnp.repeat(draws, dims[axis_at] // shards_of).reshape([-1 if axis == axis_at else 1 for axis in range(len(dims))])
    return factor_of


def split_up(count, total, most, lean):
    weights = [(1 << 20) // math.isqrt(rank ** lean) + 1 for rank in range(2, count + 1)]
    spare, given = total - most - (count - 1), [1] * (count - 1)
    while spare > 0:
        movable = [i for i in range(count - 1) if given[i] < most]
        pool, budget = sum([weights[i] for i in movable]), spare
        for i in movable:
            addition = min(most - given[i], max(1, budget * weights[i] // pool), spare)
            given[i] = given[i] + addition
            spare = spare - addition
    return np.array([most] + given)


def uneven_parts(own_key, number_of, total, most, skew):
    if number_of == 2:
        one = jax.random.randint(own_key, (), max(1, total - most), min(most, total - 1) + 1)
        return jnp.stack([one, total - one])
    lengths = jnp.asarray(split_up(number_of, total, most, skew), jnp.int32)
    couples = (number_of - 1) // 2
    giver, taker = lengths[1:1 + 2 * couples:2], lengths[2:2 + 2 * couples:2]
    margin = jnp.minimum(giver - 1, most - taker)
    shifted = jax.random.randint(jax.random.fold_in(own_key, 1), (couples,), 0, 1 << 20) % (margin + 1)
    lengths = lengths.at[1:1 + 2 * couples:2].set(giver - shifted).at[2:2 + 2 * couples:2].set(taker + shifted)
    return lengths[jax.random.permutation(jax.random.fold_in(own_key, 2), number_of)]


def scatter_about(stream_key, extent, scale, most, split=(), held_as=jnp.bfloat16):
    result = scale * jax.random.normal(stream_key, extent, jnp.float32)
    if split:
        result = result * level_of(stream_key, extent, split, -0.22, 0.18)
    return jnp.clip(result, -most, most).astype(held_as)


def setup_inputs(seed: int = 0) -> dict:
    splits = jax.random.split(jax.random.key(seed), 15)
    return {
        "layer_input": scatter_about(splits[0], (ROWS, LEN, D), 1.0, 6.0, ((0, 4), (1, 8))),
        "segment_ids": jax.vmap(lambda own: jnp.searchsorted(jnp.cumsum(uneven_parts(own, SEGS, LEN, LEN // 2, 2)), jnp.arange(LEN), side="right"))(jax.random.split(splits[1], ROWS)).reshape((ROWS, LEN)).astype(jnp.int32),
        "first_gain": jnp.clip(1.0 + 0.1 * jax.random.normal(splits[2], (D,), jnp.float32), 0.5, 1.5).astype(jnp.bfloat16),
        "query_down": scatter_about(splits[3], (D, DQ), D ** -0.5, 0.125, ((0, 32),)),
        "query_gain": jnp.clip(1.0 + 0.1 * jax.random.normal(splits[4], (DQ,), jnp.float32), 0.5, 1.5).astype(jnp.bfloat16),
        "query_up": scatter_about(splits[5], (DQ, HEADS * HEAD), DQ ** -0.5, 0.1875, ((0, 32),)),
        "key_proj": scatter_about(splits[6], (D, HEAD), D ** -0.5, 0.125, ((0, 32),)),
        "value_proj": scatter_about(splits[7], (D, HEAD), D ** -0.5, 0.125, ((0, 32),)),
        "out_proj": scatter_about(splits[8], (HEADS * HEAD, D), (max(HEADS * HEAD * 16 // LEN, 1)) ** -0.5, 0.75, ((0, 32),)),
        "second_gain": jnp.clip(1.0 + 0.1 * jax.random.normal(splits[9], (D,), jnp.float32), 0.5, 1.5).astype(jnp.bfloat16),
        "w_gate": scatter_about(splits[10], (D, FF), D ** -0.5, 0.125, ((1, 8),)),
        "w_up": scatter_about(splits[11], (D, FF), D ** -0.5, 0.125, ((1, 8),)),
        "w_down": scatter_about(splits[12], (FF, D), FF ** -0.5, 0.078125, ((0, 8),)),
        "cotangent": scatter_about(splits[13], (ROWS, LEN, D), 1.0, 6.0, ((0, 4), (1, 8))),
    }


@jax.custom_vjp
def low(v):
    return lax.optimization_barrier(v.astype(jnp.bfloat16)).astype(jnp.float32)

@jax.custom_vjp
def low_back(v):
    return v

def low_keep(v):
    return (low(v), None)

def low_pass(kept, grad):
    return (grad,)

def back_keep(v):
    return (v, None)

def back_low(kept, grad):
    return (low(grad),)
low.defvjp(low_keep, low_pass)
low_back.defvjp(back_keep, back_low)
epsilon = 1e-06
highest = lax.Precision.HIGHEST

def norm_apply(data_rows, gain_vec):
    inverse_rms = lax.rsqrt(lax.optimization_barrier(jnp.mean(data_rows * data_rows, -1, keepdims=True)) + epsilon)
    return data_rows * inverse_rms * gain_vec

def rotate(data_rows, cosine_table, sine_table):
    half_size = data_rows.shape[-1] // 2
    turned = jnp.concatenate([-data_rows[..., half_size:], data_rows[..., :half_size]], -1)
    return data_rows * cosine_table + turned * sine_table

def angle_tables(positions, head_size):
    frequency = 10000.0 ** (-jnp.arange(0, head_size, 2).astype(jnp.float32) / head_size)
    angles = positions.astype(jnp.float32)[:, None] * frequency[None, :]
    angles = jnp.concatenate([angles, angles], -1)
    return (jnp.cos(angles), jnp.sin(angles))

def matmul(left_op, right_op):
    return jnp.dot(left_op, right_op, precision=highest, preferred_element_type=jnp.float32)

def row_forward(inputs, segment_row, params):
    gain_first, down_query, gain_query, up_query, key_weights, value_weights, out_weights, gain_second, gate_weights, up_weights, down_weights = params
    length = inputs.shape[0]
    positions = jnp.arange(length).astype(jnp.int32)
    cosine_table, sine_table = angle_tables(positions, HEAD)
    normed_in = low(norm_apply(inputs, gain_first))
    query_low = low_back(matmul(normed_in, down_query))
    query_norm = low(norm_apply(query_low, gain_query))
    query_raw = low_back(matmul(query_norm, up_query)).reshape(length, HEADS, HEAD)
    queries = low(rotate(query_raw, cosine_table[:, None, :], sine_table[:, None, :]))
    key_rows = low(rotate(low_back(matmul(normed_in, key_weights)), cosine_table, sine_table))
    value_rows = low(low_back(matmul(normed_in, value_weights)))
    block_rows = min(512, length)
    block_count = length // block_rows

    def one_block(pieces):
        query_block, pos_block, seg_block = pieces
        logits = jnp.einsum('thd,sd->ths', query_block, key_rows, precision=highest) * HEAD ** (-0.5)
        logits = low_back(logits)
        allowed = (positions[None, :] <= pos_block[:, None]) & (segment_row[None, :] == seg_block[:, None])
        masked = jnp.where(allowed[:, None, :], logits, -1e+30)
        attention = low(jax.nn.softmax(masked, axis=-1))
        return jnp.einsum('ths,sd->thd', attention, value_rows, precision=highest)
    attended = lax.map(jax.checkpoint(one_block), (queries.reshape(block_count, block_rows, HEADS, HEAD), positions.reshape(block_count, block_rows), segment_row.reshape(block_count, block_rows)))
    attended = low(low_back(attended.reshape(length, HEADS * HEAD)))
    mid_sum = inputs + low_back(matmul(attended, out_weights))
    normed_mid = low(norm_apply(mid_sum, gain_second))
    gate_pre = low_back(matmul(normed_mid, gate_weights))
    up_pre = low_back(matmul(normed_mid, up_weights))
    hidden = low(jax.nn.silu(gate_pre) * up_pre)
    return mid_sum + low_back(matmul(hidden, down_weights))

def reference(layer_input, segment_ids, first_gain, query_down, query_gain, query_up, key_proj, value_proj, out_proj, second_gain, w_gate, w_up, w_down, cotangent):
    params = tuple((weight_item.astype(jnp.float32) for weight_item in (first_gain, query_down, query_gain, query_up, key_proj, value_proj, out_proj, second_gain, w_gate, w_up, w_down)))
    inputs = layer_input.astype(jnp.float32)

    def layer_forward(all_inputs, all_params):

        def row_step(carried, pieces):
            return (carried, row_forward(pieces[0], pieces[1], all_params))
        carried, outputs = lax.scan(row_step, None, (all_inputs, segment_ids))
        return outputs
    outputs, pullback = jax.vjp(layer_forward, inputs, params)
    grad_input, weight_grads = pullback(cotangent.astype(jnp.float32))
    return (outputs, grad_input, weight_grads[0], weight_grads[1], weight_grads[2], weight_grads[3], weight_grads[4], weight_grads[5], weight_grads[6], weight_grads[7], weight_grads[8], weight_grads[9], weight_grads[10])
```

```python
import functools

import jax
import jax.numpy as jnp
from jax import lax
from jax.sharding import PartitionSpec as P

HEADS = 16
HEAD = 256


epsilon = 1e-06
masked_value = -1e30


def norm_apply(data_rows, gain_vec):
    inverse_rms = lax.rsqrt(jnp.mean(data_rows * data_rows, -1, keepdims=True) + epsilon)
    return data_rows * inverse_rms * gain_vec


def rotate(data_rows, cosine_table, sine_table):
    half_size = data_rows.shape[-1] // 2
    turned = jnp.concatenate([-data_rows[..., half_size:], data_rows[..., :half_size]], -1)
    return data_rows * cosine_table + turned * sine_table


def angle_tables(positions, head_size):
    frequency = 10000.0 ** (-jnp.arange(0, head_size, 2).astype(jnp.float32) / head_size)
    angles = positions.astype(jnp.float32)[:, None] * frequency[None, :]
    angles = jnp.concatenate([angles, angles], -1)
    return (jnp.cos(angles), jnp.sin(angles))


def matmul(left_op, right_op):
    return jnp.dot(left_op, right_op, preferred_element_type=jnp.float32)


def dot_across(left_op, right_op):
    return lax.dot_general(
        left_op, right_op, (((0,), (0,)), ((), ())), preferred_element_type=jnp.float32
    )


def dot_transposed(left_op, right_op):
    return lax.dot_general(
        left_op, right_op, (((1,), (1,)), ((), ())), preferred_element_type=jnp.float32
    )


def gather_layer(
    first_gain, query_down, query_gain, query_up, key_proj, value_proj, out_proj, second_gain
):
    return (
        lax.all_gather(first_gain, ("dp", "seq"), axis=0, tiled=True),
        lax.all_gather(query_down, ("dp", "seq"), axis=0, tiled=True),
        lax.all_gather(query_gain, ("dp", "seq"), axis=0, tiled=True),
        lax.all_gather(query_up, ("dp", "seq"), axis=0, tiled=True),
        lax.all_gather(key_proj, ("dp", "seq"), axis=0, tiled=True),
        lax.all_gather(value_proj, ("dp", "seq"), axis=0, tiled=True),
        lax.all_gather(out_proj, ("dp", "seq"), axis=0, tiled=True),
        lax.all_gather(second_gain, ("dp", "seq"), axis=0, tiled=True),
    )


def front_pass(inputs, segment_row, weights_all, positions, cosine_table, sine_table):
    (
        gain_first,
        down_query,
        gain_query,
        up_query,
        key_weights,
        value_weights,
        out_weights,
        gain_second,
    ) = weights_all
    tok_rows = inputs.shape[0]
    normed_in = norm_apply(inputs, gain_first.astype(jnp.float32)).astype(jnp.bfloat16)
    query_low = matmul(normed_in, down_query)
    query_norm = norm_apply(query_low, gain_query.astype(jnp.float32)).astype(jnp.bfloat16)
    query_raw = matmul(query_norm, up_query).reshape(tok_rows, HEADS, HEAD)
    queries = rotate(query_raw, cosine_table[:, None, :], sine_table[:, None, :]).astype(
        jnp.bfloat16
    )
    key_own = rotate(matmul(normed_in, key_weights), cosine_table, sine_table).astype(jnp.bfloat16)
    value_own = matmul(normed_in, value_weights).astype(jnp.bfloat16)
    key_value = jnp.concatenate([key_own, value_own], -1)
    kv_all = lax.all_gather(key_value, "seq", axis=0, tiled=True)
    own_segments = lax.dynamic_slice_in_dim(segment_row, positions[0], tok_rows, 0)
    all_positions = jnp.arange(segment_row.shape[0], dtype=jnp.int32)
    allowed = (all_positions[None, :] <= positions[:, None]) & (
        segment_row[None, :] == own_segments[:, None]
    )
    logits = jnp.einsum(
        "thd,sd->ths", queries, kv_all[:, :HEAD], preferred_element_type=jnp.float32
    ) * HEAD ** (-0.5)
    masked = jnp.where(allowed[:, None, :], logits, masked_value)
    attention = jax.nn.softmax(masked, axis=-1)
    attended = jnp.einsum(
        "ths,sd->thd",
        attention.astype(jnp.bfloat16),
        kv_all[:, HEAD:],
        preferred_element_type=jnp.float32,
    )
    attended = attended.reshape(tok_rows, HEADS * HEAD).astype(jnp.bfloat16)
    mid_sum = inputs + matmul(attended, out_weights)
    normed_mid = norm_apply(mid_sum, gain_second.astype(jnp.float32)).astype(jnp.bfloat16)
    return (
        normed_in,
        query_low,
        query_norm,
        queries,
        kv_all,
        attention,
        attended,
        mid_sum,
        normed_mid,
    )


def feed_front(normed_mid, w_gate, w_up):
    normed_all = lax.all_gather(normed_mid, "seq", axis=0, tiled=True)
    return feed_local(normed_all, w_gate, w_up)


def feed_local(normed_rows_in, gate_weights, up_weights):
    gate_pre = matmul(normed_rows_in, gate_weights)
    up_pre = matmul(normed_rows_in, up_weights)
    hidden = (jax.nn.silu(gate_pre) * up_pre).astype(jnp.bfloat16)
    return (normed_rows_in, gate_pre, up_pre, hidden)


def gated_unit(gate_in, up_in):
    return jax.nn.silu(gate_in) * up_in


def local_tokens(
    layer_input,
    segment_ids,
    first_gain,
    query_down,
    query_gain,
    query_up,
    key_proj,
    value_proj,
    out_proj,
    second_gain,
    w_gate,
    w_up,
    w_down,
    cotangent,
):
    inputs = layer_input[0].astype(jnp.float32)
    segment_row = segment_ids[0]
    tok_rows = inputs.shape[0]
    positions = lax.axis_index("seq") * tok_rows + jnp.arange(tok_rows, dtype=jnp.int32)
    cosine_table, sine_table = angle_tables(positions, HEAD)
    weights_all = gather_layer(
        first_gain, query_down, query_gain, query_up, key_proj, value_proj, out_proj, second_gain
    )
    stored_front = front_pass(inputs, segment_row, weights_all, positions, cosine_table, sine_table)
    feed_state = feed_front(stored_front[8], w_gate, w_up)
    hidden_now = feed_state[3]
    branch_out = lax.psum_scatter(
        matmul(hidden_now, w_down), "seq", scatter_dimension=0, tiled=True
    )
    layer_out = stored_front[7] + branch_out
    weights_all = gather_layer(
        first_gain, query_down, query_gain, query_up, key_proj, value_proj, out_proj, second_gain
    )
    stored_front = front_pass(inputs, segment_row, weights_all, positions, cosine_table, sine_table)
    feed_state = feed_front(stored_front[8], w_gate, w_up)
    (
        gain_first,
        down_query,
        gain_query,
        up_query,
        key_weights,
        value_weights,
        out_weights,
        gain_second,
    ) = weights_all
    normed_in, query_low, query_norm, queries, kv_all, attention, attended, mid_sum, normed_mid = (
        stored_front
    )
    normed_all, gate_pre, up_pre, hidden = feed_state
    cot_rows = cotangent[0]
    piece_rows = lax.all_gather(cot_rows, "seq", axis=0, tiled=True)
    down_grad = dot_across(hidden, piece_rows)
    grad_hidden = dot_transposed(piece_rows, w_down)
    gated_value, gate_pull = jax.vjp(gated_unit, gate_pre, up_pre)
    gate_grad, up_grad = gate_pull(grad_hidden)
    gate_grad = gate_grad.astype(jnp.bfloat16)
    up_grad = up_grad.astype(jnp.bfloat16)
    gating_grad = dot_across(normed_all, gate_grad)
    upward_grad = dot_across(normed_all, up_grad)
    normed_grad = lax.psum_scatter(
        dot_transposed(gate_grad, w_gate) + dot_transposed(up_grad, w_up),
        "seq",
        scatter_dimension=0,
        tiled=True,
    )
    feed_grads = lax.psum((gating_grad, upward_grad, down_grad), "dp")
    norm_value, second_pull = jax.vjp(norm_apply, mid_sum, gain_second.astype(jnp.float32))
    mid_grad, second_grad = second_pull(normed_grad)
    mid_grad = mid_grad + cot_rows.astype(jnp.float32)
    attn_grad = mid_grad.astype(jnp.bfloat16)
    output_grad = dot_across(attended, attn_grad)
    context_grad = (
        dot_transposed(attn_grad, out_weights).astype(jnp.bfloat16).reshape(tok_rows, HEADS, HEAD)
    )
    key_all = kv_all[:, :HEAD]
    value_all = kv_all[:, HEAD:]
    scale_value = HEAD ** (-0.5)
    probs_grad = jnp.einsum(
        "thd,sd->ths", context_grad, value_all, preferred_element_type=jnp.float32
    )
    inner_sum = jnp.sum(attention * probs_grad, -1, keepdims=True)
    logit_grad = (attention * (probs_grad - inner_sum)).astype(jnp.bfloat16)
    queries_grad = (
        jnp.einsum("ths,sd->thd", logit_grad, key_all, preferred_element_type=jnp.float32)
        * scale_value
    )
    keys_grad = (
        jnp.einsum("ths,thd->sd", logit_grad, queries, preferred_element_type=jnp.float32)
        * scale_value
    )
    values_grad = jnp.einsum(
        "ths,thd->sd",
        attention.astype(jnp.bfloat16),
        context_grad,
        preferred_element_type=jnp.float32,
    )
    kv_grads = lax.psum_scatter(
        jnp.concatenate([keys_grad, values_grad], -1), "seq", scatter_dimension=0, tiled=True
    )
    key_grad = rotate(kv_grads[:, :HEAD], cosine_table, -sine_table).astype(jnp.bfloat16)
    value_grad = kv_grads[:, HEAD:].astype(jnp.bfloat16)
    query_grad = rotate(queries_grad, cosine_table[:, None, :], -sine_table[:, None, :])
    query_grad = query_grad.reshape(tok_rows, HEADS * HEAD).astype(jnp.bfloat16)
    lifted_grad = dot_across(query_norm, query_grad)
    compact_grad = dot_transposed(query_grad, up_query)
    query_value, query_pull = jax.vjp(norm_apply, query_low, gain_query.astype(jnp.float32))
    latent_grad, compact_gain = query_pull(compact_grad)
    latent_grad = latent_grad.astype(jnp.bfloat16)
    compress_grad = dot_across(normed_in, latent_grad)
    keymap_grad = dot_across(normed_in, key_grad)
    valuemap_grad = dot_across(normed_in, value_grad)
    entry_grad = (
        dot_transposed(latent_grad, down_query)
        + dot_transposed(key_grad, key_weights)
        + dot_transposed(value_grad, value_weights)
    )
    first_value, first_pull = jax.vjp(norm_apply, inputs, gain_first.astype(jnp.float32))
    inputs_grad, first_grad = first_pull(entry_grad)
    inputs_grad = inputs_grad + mid_grad
    layer_grads = (
        lax.psum_scatter(first_grad, ("dp", "seq"), scatter_dimension=0, tiled=True),
        lax.psum_scatter(compress_grad, ("dp", "seq"), scatter_dimension=0, tiled=True),
        lax.psum_scatter(compact_gain, ("dp", "seq"), scatter_dimension=0, tiled=True),
        lax.psum_scatter(lifted_grad, ("dp", "seq"), scatter_dimension=0, tiled=True),
        lax.psum_scatter(keymap_grad, ("dp", "seq"), scatter_dimension=0, tiled=True),
        lax.psum_scatter(valuemap_grad, ("dp", "seq"), scatter_dimension=0, tiled=True),
        lax.psum_scatter(output_grad, ("dp", "seq"), scatter_dimension=0, tiled=True),
        lax.psum_scatter(second_grad, ("dp", "seq"), scatter_dimension=0, tiled=True),
    )
    return (
        layer_out[None],
        inputs_grad[None],
        layer_grads[0],
        layer_grads[1],
        layer_grads[2],
        layer_grads[3],
        layer_grads[4],
        layer_grads[5],
        layer_grads[6],
        layer_grads[7],
        feed_grads[0],
        feed_grads[1],
        feed_grads[2],
    )


def local_heads(
    row_count,
    seq_count,
    layer_input,
    segment_ids,
    first_gain,
    query_down,
    query_gain,
    query_up,
    key_proj,
    value_proj,
    out_proj,
    second_gain,
    w_gate,
    w_up,
    w_down,
    cotangent,
):
    f32, bf16 = jnp.float32, jnp.bfloat16
    seq_at = lax.axis_index("seq")
    core_at = lax.rem(seq_at, 2)
    swap = [(i, i ^ 1) for i in range(seq_count)]
    own_rows = layer_input.shape[1]
    length = own_rows * seq_count
    width = layer_input.shape[2]
    low_width = query_down.shape[1]
    down_rows = query_down.shape[0]
    up_rows = query_up.shape[0]
    out_rows = out_proj.shape[0]
    half_count = row_count // 2
    chips = seq_count // 2
    own_low = low_width // seq_count
    low_part = own_low // row_count
    kv_parts = seq_count // 2
    kv_rows = length // kv_parts
    kv_at = lax.rem(seq_at, kv_parts)
    is_key = seq_at < kv_parts
    spare = 8
    own_heads = half_count

    gains = jnp.zeros((spare, own_low + HEAD), bf16)
    gains = gains.at[0, :down_rows].set(first_gain)
    gains = gains.at[1, :down_rows].set(second_gain)
    gains = gains.at[2, :up_rows].set(query_gain)
    low_cols = query_down.reshape(down_rows, row_count, seq_count, low_part)
    low_cols = low_cols.transpose(2, 0, 1, 3).reshape(seq_count, down_rows, own_low)
    kv_cols = jnp.stack([key_proj] * kv_parts + [value_proj] * kv_parts)
    sent = jnp.concatenate([low_cols, kv_cols], -1)
    sent = jnp.concatenate(
        [sent, jnp.broadcast_to(gains[None], (seq_count, spare, own_low + HEAD))], 1
    )
    sent = sent.reshape(seq_count * (down_rows + spare), own_low + HEAD)
    sent = lax.all_to_all(sent, "seq", 0, 0, tiled=True)
    entry_all = lax.all_gather(sent, "dp", axis=0, tiled=True)
    entry_all = entry_all.reshape(row_count * seq_count, down_rows + spare, own_low + HEAD)
    entry_weights = entry_all[:, :down_rows].reshape(width, own_low + HEAD)
    gain_first = entry_all[:, down_rows, :down_rows].reshape(width).astype(f32)
    gain_second = entry_all[:, down_rows + 1, :down_rows].reshape(width).astype(f32)
    gain_query = entry_all[:, down_rows + 2, :up_rows].reshape(row_count, seq_count, low_part)
    gain_query = gain_query.transpose(1, 0, 2).reshape(low_width).astype(f32)

    inputs_all = lax.all_gather(layer_input[0], "seq", axis=0, tiled=True)

    up_sent = query_up.reshape(up_rows, 2, half_count, chips, HEAD).transpose(3, 1, 0, 2, 4)
    up_sent = up_sent.reshape(seq_count * up_rows, own_heads * HEAD)
    up_mine = lax.all_to_all(up_sent, "seq", 0, 0, tiled=True)
    up_mine = lax.all_gather(up_mine, "dp", axis=0, tiled=True)
    up_mine = up_mine.reshape(row_count, seq_count, low_part, own_heads * HEAD)
    up_mine = up_mine.transpose(1, 0, 2, 3).reshape(low_width, own_heads * HEAD)

    out_all = lax.all_gather(out_proj, "dp", axis=0, tiled=False)
    out_kept = lax.dynamic_slice_in_dim(out_all, core_at * half_count, half_count, 0)
    out_given = lax.dynamic_slice_in_dim(out_all, (1 - core_at) * half_count, half_count, 0)
    out_got = lax.ppermute(out_given, "seq", swap)
    out_mine = jnp.where(
        core_at == 0,
        jnp.stack([out_kept, out_got], 1),
        jnp.stack([out_got, out_kept], 1),
    ).reshape(own_heads * HEAD, width)

    cot_rows = cotangent[0]
    cot_all = lax.all_gather(cot_rows, "seq", axis=0, tiled=True)

    positions = jnp.arange(length, dtype=jnp.int32)
    cosine_table, sine_table = angle_tables(positions, HEAD)

    inputs_wide = inputs_all.astype(f32)
    entry_scale = lax.rsqrt(jnp.mean(inputs_wide * inputs_wide, -1, keepdims=True) + epsilon)
    normed_in = (inputs_wide * entry_scale * gain_first).astype(bf16)
    low_own = matmul(normed_in, entry_weights)
    kv_own = lax.dynamic_slice_in_dim(low_own[:, own_low:], kv_at * kv_rows, kv_rows, 0)
    kv_cos = lax.dynamic_slice_in_dim(cosine_table, kv_at * kv_rows, kv_rows, 0)
    kv_sin = lax.dynamic_slice_in_dim(sine_table, kv_at * kv_rows, kv_rows, 0)
    kv_own = jnp.where(is_key, rotate(kv_own, kv_cos, kv_sin), kv_own).astype(bf16)
    half_head = HEAD // 2
    low_sent = jnp.concatenate(
        [low_own[:, :own_low].astype(bf16), kv_own[:, :half_head], kv_own[:, half_head:]], 0
    )
    low_all = lax.all_gather(low_sent, "seq", axis=0, tiled=False)
    query_low = low_all[:, :length].transpose(1, 0, 2).reshape(length, low_width).astype(f32)
    kv_all = jnp.concatenate(
        [low_all[:, length : length + kv_rows], low_all[:, length + kv_rows :]], -1
    )
    key_all = kv_all[:kv_parts].reshape(length, HEAD)
    value_all = kv_all[kv_parts:].reshape(length, HEAD)

    query_scale = lax.rsqrt(jnp.mean(query_low * query_low, -1, keepdims=True) + epsilon)
    query_norm = (query_low * query_scale * gain_query).astype(bf16)
    query_raw = matmul(query_norm, up_mine).reshape(length, own_heads, HEAD)
    queries = rotate(query_raw, cosine_table[:, None, :], sine_table[:, None, :]).astype(bf16)
    queries = queries.transpose(1, 0, 2)
    segment_row = segment_ids[0]
    allowed = (positions[None, :] <= positions[:, None]) & (
        segment_row[None, :] == segment_row[:, None]
    )
    scale_value = HEAD ** (-0.5)
    logits = (
        jnp.einsum("htd,sd->hts", queries, key_all, preferred_element_type=f32) * scale_value
    )
    masked = jnp.where(allowed[None], logits, masked_value)
    attention = jax.nn.softmax(masked, axis=-1)
    attention_low = attention.astype(bf16)
    attended = jnp.einsum("hts,sd->htd", attention_low, value_all, preferred_element_type=f32)
    attended = attended.astype(bf16).transpose(1, 0, 2).reshape(length, own_heads * HEAD)
    mixed = matmul(attended, out_mine).astype(bf16)
    mixed = lax.psum_scatter(mixed, "seq", scatter_dimension=0, tiled=True).astype(f32)
    mid_sum = layer_input[0].astype(f32) + mixed
    mid_scale = lax.rsqrt(jnp.mean(mid_sum * mid_sum, -1, keepdims=True) + epsilon)
    mid_unit = mid_sum * mid_scale
    normed_mid = (mid_unit * gain_second).astype(bf16)

    normed_all = lax.all_gather(normed_mid, "seq", axis=0, tiled=True)
    grad_hidden = dot_transposed(cot_all, w_down)
    gate_pre = matmul(normed_all, w_gate)
    up_pre = matmul(normed_all, w_up)
    hidden = gated_unit(gate_pre, up_pre)
    gated_value, gate_pull = jax.vjp(gated_unit, gate_pre, up_pre)
    hidden = gated_value.astype(bf16)
    gate_grad, up_grad = gate_pull(grad_hidden)
    gate_grad = gate_grad.astype(bf16)
    up_grad = up_grad.astype(bf16)
    normed_grad = dot_transposed(gate_grad, w_gate) + dot_transposed(up_grad, w_up)
    normed_grad = lax.psum_scatter(
        normed_grad.astype(bf16), "seq", scatter_dimension=0, tiled=True
    ).astype(f32)
    down_grad = dot_across(hidden, cot_all).astype(bf16)
    gating_grad = dot_across(normed_all, gate_grad).astype(bf16)
    upward_grad = dot_across(normed_all, up_grad).astype(bf16)
    feed_grads = lax.psum((gating_grad, upward_grad, down_grad), "dp")
    branch_out = lax.psum_scatter(
        matmul(hidden, w_down).astype(bf16), "seq", scatter_dimension=0, tiled=True
    )
    layer_out = mid_sum + branch_out.astype(f32)

    second_grad = jnp.sum(normed_grad * mid_unit, 0)
    scaled_grad = normed_grad * gain_second
    mid_grad = mid_scale * (
        scaled_grad - mid_unit * jnp.mean(scaled_grad * mid_unit, -1, keepdims=True)
    )
    mid_grad = mid_grad + cot_rows.astype(f32)
    attn_grad = lax.all_gather(mid_grad.astype(bf16), "seq", axis=0, tiled=True)

    context_grad = dot_transposed(attn_grad, out_mine).astype(bf16)
    context_grad = context_grad.reshape(length, own_heads, HEAD).transpose(1, 0, 2)
    probs_grad = jnp.einsum("htd,sd->hts", context_grad, value_all, preferred_element_type=f32)
    inner_sum = jnp.sum(attention * probs_grad, -1, keepdims=True)
    logit_grad = (attention * (probs_grad - inner_sum)).astype(bf16)
    queries_grad = (
        jnp.einsum("hts,sd->htd", logit_grad, key_all, preferred_element_type=f32) * scale_value
    )
    keys_grad = (
        jnp.einsum("hts,htd->sd", logit_grad, queries, preferred_element_type=f32) * scale_value
    )
    values_grad = jnp.einsum(
        "hts,htd->sd", attention_low, context_grad, preferred_element_type=f32
    )
    query_grad = rotate(queries_grad, cosine_table, -sine_table).astype(bf16)
    query_grad = query_grad.transpose(1, 0, 2).reshape(length, own_heads * HEAD)
    compact_grad = dot_transposed(query_grad, up_mine)
    query_unit = query_low * query_scale
    compact_mean = jnp.sum(compact_grad * gain_query * query_unit, -1) / low_width
    mean_rows = compact_mean.reshape(length // own_low, own_low)
    compact_sent = compact_grad.astype(bf16).reshape(length, seq_count, own_low).transpose(1, 0, 2)
    kv_sent = jnp.concatenate([keys_grad, values_grad], 0).astype(bf16)
    kv_sent = kv_sent.reshape(seq_count, kv_rows, HEAD)
    mean_high = mean_rows.astype(bf16)
    mean_low = (mean_rows - mean_high.astype(f32)).astype(bf16)
    means = jnp.broadcast_to(
        jnp.concatenate([mean_high, mean_low], 0)[None],
        (seq_count, 2 * mean_rows.shape[0], own_low),
    )
    back_sent = jnp.concatenate(
        [compact_sent, kv_sent[:, :, :half_head], kv_sent[:, :, half_head:], means], 1
    )
    back = lax.psum_scatter(back_sent, "seq", scatter_dimension=0, tiled=False).astype(f32)

    output_grad = dot_across(attended, attn_grad).astype(bf16)
    output_grad = output_grad.reshape(own_heads, 2, out_rows, width)
    grad_kept = lax.dynamic_index_in_dim(output_grad, core_at, 1, False)
    grad_given = lax.dynamic_index_in_dim(output_grad, 1 - core_at, 1, False)
    grad_got = lax.ppermute(grad_given, "seq", swap)
    output_grad = jnp.where(
        core_at == 0,
        jnp.concatenate([grad_kept, grad_got], 0),
        jnp.concatenate([grad_got, grad_kept], 0),
    )
    output_grad = lax.psum_scatter(output_grad, "dp", scatter_dimension=0, tiled=False)

    lifted_grad = dot_across(query_norm, query_grad).astype(bf16)
    lifted_grad = lifted_grad.reshape(seq_count, row_count, up_rows, own_heads * HEAD)
    lifted_grad = lifted_grad.transpose(1, 0, 2, 3)
    lifted_grad = lifted_grad.reshape(row_count * seq_count * up_rows, own_heads * HEAD)
    lifted_grad = lax.psum_scatter(lifted_grad, "dp", scatter_dimension=0, tiled=True)
    lifted_grad = lax.all_to_all(lifted_grad, "seq", 0, 0, tiled=True)
    lifted_grad = lifted_grad.reshape(chips, 2, up_rows, half_count, HEAD)
    lifted_grad = lifted_grad.transpose(2, 1, 3, 0, 4).reshape(up_rows, HEADS * HEAD)

    compact_own = back[:length]
    kv_back = jnp.concatenate(
        [back[length : length + kv_rows], back[length + kv_rows : length + 2 * kv_rows]], -1
    )
    mean_back = back[length + 2 * kv_rows :].reshape(2, length).sum(0)[:, None]
    low_at = seq_at * own_low
    unit_own = lax.dynamic_slice_in_dim(query_unit, low_at, own_low, 1)
    gain_own = lax.dynamic_slice_in_dim(gain_query, low_at, own_low, 0)
    compact_gain = jnp.sum(compact_own * unit_own, 0)
    latent_grad = (query_scale * (compact_own * gain_own - unit_own * mean_back)).astype(bf16)
    kv_back = jnp.where(is_key, rotate(kv_back, kv_cos, -kv_sin), kv_back).astype(bf16)
    kv_padded = lax.dynamic_update_slice_in_dim(
        jnp.zeros((length, HEAD), bf16), kv_back, kv_at * kv_rows, 0
    )
    entry_sent = jnp.concatenate([latent_grad, kv_padded], -1)
    entry_part = dot_transposed(entry_sent, entry_weights)
    entry_grad = lax.psum_scatter(
        entry_part.astype(bf16), "seq", scatter_dimension=0, tiled=True
    ).astype(f32)
    first_grad = jnp.sum(entry_part * (inputs_wide * entry_scale), 0)
    own_at = seq_at * own_rows
    inputs_own = layer_input[0].astype(f32)
    scale_own = lax.dynamic_slice_in_dim(entry_scale, own_at, own_rows, 0)
    entry_unit = inputs_own * scale_own
    entry_scaled = entry_grad * gain_first
    inputs_grad = scale_own * (
        entry_scaled - entry_unit * jnp.mean(entry_scaled * entry_unit, -1, keepdims=True)
    )
    inputs_grad = inputs_grad + mid_grad

    blocks = row_count * seq_count
    weight_grad = dot_across(normed_in, entry_sent).astype(bf16)
    weight_grad = weight_grad.reshape(blocks, down_rows, own_low + HEAD)
    mine = (jnp.arange(seq_count) == seq_at)[None, :, None]
    gain_back = jnp.where(mine, compact_gain.reshape(row_count, 1, low_part), 0.0)
    extra = jnp.zeros((blocks, spare, own_low + HEAD), f32)
    extra = extra.at[:, 0, :down_rows].set(first_grad.reshape(blocks, down_rows))
    extra = extra.at[:, 1, :down_rows].set(second_grad.reshape(blocks, down_rows))
    extra = extra.at[:, 2, :low_part].set(gain_back.reshape(blocks, low_part))
    weight_grad = jnp.concatenate([weight_grad, extra.astype(bf16)], 1)
    weight_grad = weight_grad.reshape(blocks * (down_rows + spare), own_low + HEAD)
    weight_grad = lax.psum_scatter(weight_grad, "dp", scatter_dimension=0, tiled=True)
    weight_grad = lax.all_to_all(weight_grad, "seq", 0, 0, tiled=True).astype(f32)
    weight_grad = weight_grad.reshape(seq_count, down_rows + spare, own_low + HEAD)
    compress_grad = weight_grad[:, :down_rows, :own_low].reshape(
        seq_count, down_rows, row_count, low_part
    )
    compress_grad = compress_grad.transpose(1, 2, 0, 3).reshape(down_rows, low_width)
    keymap_grad = jnp.sum(weight_grad[:kv_parts, :down_rows, own_low:], 0)
    valuemap_grad = jnp.sum(weight_grad[kv_parts:, :down_rows, own_low:], 0)
    gain_rows = jnp.sum(weight_grad[:, down_rows:], 0)
    return (
        layer_out[None],
        inputs_grad[None],
        gain_rows[0, :down_rows],
        compress_grad,
        gain_rows[2, :low_part],
        lifted_grad.astype(f32),
        keymap_grad,
        valuemap_grad,
        output_grad.astype(f32),
        gain_rows[1, :down_rows],
        feed_grads[0].astype(f32),
        feed_grads[1].astype(f32),
        feed_grads[2].astype(f32),
    )


def solution(mesh):
    row_count, seq_count = mesh.shape["dp"], mesh.shape["seq"]
    if row_count % 2 == 0 and seq_count % 2 == 0 and HEADS * 2 == row_count * seq_count:
        local = functools.partial(local_heads, row_count, seq_count)
    else:
        local = local_tokens
    return jax.shard_map(
        local,
        mesh=mesh,
        in_specs=(
            P("dp", "seq", None),
            P("dp", None),
            P(("dp", "seq")),
            P(("dp", "seq"), None),
            P(("dp", "seq")),
            P(("dp", "seq"), None),
            P(("dp", "seq"), None),
            P(("dp", "seq"), None),
            P(("dp", "seq"), None),
            P(("dp", "seq")),
            P(None, "seq"),
            P(None, "seq"),
            P("seq", None),
            P("dp", "seq", None),
        ),
        out_specs=(
            P("dp", "seq", None),
            P("dp", "seq", None),
            P(("dp", "seq")),
            P(("dp", "seq"), None),
            P(("dp", "seq")),
            P(("dp", "seq"), None),
            P(("dp", "seq"), None),
            P(("dp", "seq"), None),
            P(("dp", "seq"), None),
            P(("dp", "seq")),
            P(None, "seq"),
            P(None, "seq"),
            P("seq", None),
        ),
        check_vma=False,
    )
```

```python
import functools

import jax
import jax.numpy as jnp
from jax import lax
from jax.experimental import pallas as pl
from jax.experimental.pallas import tpu as pltpu
from jax.sharding import PartitionSpec as P

HEADS = 16
HEAD = 256


epsilon = 1e-06
masked_value = -1e30


def norm_apply(data_rows, gain_vec):
    inverse_rms = lax.rsqrt(jnp.mean(data_rows * data_rows, -1, keepdims=True) + epsilon)
    return data_rows * inverse_rms * gain_vec


def rotate(data_rows, cosine_table, sine_table):
    half_size = data_rows.shape[-1] // 2
    turned = jnp.concatenate([-data_rows[..., half_size:], data_rows[..., :half_size]], -1)
    return data_rows * cosine_table + turned * sine_table


def angle_tables(positions, head_size):
    frequency = 10000.0 ** (-jnp.arange(0, head_size, 2).astype(jnp.float32) / head_size)
    angles = positions.astype(jnp.float32)[:, None] * frequency[None, :]
    angles = jnp.concatenate([angles, angles], -1)
    return (jnp.cos(angles), jnp.sin(angles))


def matmul(left_op, right_op):
    return jnp.dot(left_op, right_op, preferred_element_type=jnp.float32)


def dot_across(left_op, right_op):
    return lax.dot_general(
        left_op, right_op, (((0,), (0,)), ((), ())), preferred_element_type=jnp.float32
    )


def dot_transposed(left_op, right_op):
    return lax.dot_general(
        left_op, right_op, (((1,), (1,)), ((), ())), preferred_element_type=jnp.float32
    )


def gather_layer(
    first_gain, query_down, query_gain, query_up, key_proj, value_proj, out_proj, second_gain
):
    return (
        lax.all_gather(first_gain, ("dp", "seq"), axis=0, tiled=True),
        lax.all_gather(query_down, ("dp", "seq"), axis=0, tiled=True),
        lax.all_gather(query_gain, ("dp", "seq"), axis=0, tiled=True),
        lax.all_gather(query_up, ("dp", "seq"), axis=0, tiled=True),
        lax.all_gather(key_proj, ("dp", "seq"), axis=0, tiled=True),
        lax.all_gather(value_proj, ("dp", "seq"), axis=0, tiled=True),
        lax.all_gather(out_proj, ("dp", "seq"), axis=0, tiled=True),
        lax.all_gather(second_gain, ("dp", "seq"), axis=0, tiled=True),
    )


def front_pass(inputs, segment_row, weights_all, positions, cosine_table, sine_table):
    (
        gain_first,
        down_query,
        gain_query,
        up_query,
        key_weights,
        value_weights,
        out_weights,
        gain_second,
    ) = weights_all
    tok_rows = inputs.shape[0]
    normed_in = norm_apply(inputs, gain_first.astype(jnp.float32)).astype(jnp.bfloat16)
    query_low = matmul(normed_in, down_query)
    query_norm = norm_apply(query_low, gain_query.astype(jnp.float32)).astype(jnp.bfloat16)
    query_raw = matmul(query_norm, up_query).reshape(tok_rows, HEADS, HEAD)
    queries = rotate(query_raw, cosine_table[:, None, :], sine_table[:, None, :]).astype(
        jnp.bfloat16
    )
    key_own = rotate(matmul(normed_in, key_weights), cosine_table, sine_table).astype(jnp.bfloat16)
    value_own = matmul(normed_in, value_weights).astype(jnp.bfloat16)
    key_value = jnp.concatenate([key_own, value_own], -1)
    kv_all = lax.all_gather(key_value, "seq", axis=0, tiled=True)
    own_segments = lax.dynamic_slice_in_dim(segment_row, positions[0], tok_rows, 0)
    all_positions = jnp.arange(segment_row.shape[0], dtype=jnp.int32)
    allowed = (all_positions[None, :] <= positions[:, None]) & (
        segment_row[None, :] == own_segments[:, None]
    )
    logits = jnp.einsum(
        "thd,sd->ths", queries, kv_all[:, :HEAD], preferred_element_type=jnp.float32
    ) * HEAD ** (-0.5)
    masked = jnp.where(allowed[:, None, :], logits, masked_value)
    attention = jax.nn.softmax(masked, axis=-1)
    attended = jnp.einsum(
        "ths,sd->thd",
        attention.astype(jnp.bfloat16),
        kv_all[:, HEAD:],
        preferred_element_type=jnp.float32,
    )
    attended = attended.reshape(tok_rows, HEADS * HEAD).astype(jnp.bfloat16)
    mid_sum = inputs + matmul(attended, out_weights)
    normed_mid = norm_apply(mid_sum, gain_second.astype(jnp.float32)).astype(jnp.bfloat16)
    return (
        normed_in,
        query_low,
        query_norm,
        queries,
        kv_all,
        attention,
        attended,
        mid_sum,
        normed_mid,
    )


def feed_front(normed_mid, w_gate, w_up):
    normed_all = lax.all_gather(normed_mid, "seq", axis=0, tiled=True)
    return feed_local(normed_all, w_gate, w_up)


def feed_local(normed_rows_in, gate_weights, up_weights):
    gate_pre = matmul(normed_rows_in, gate_weights)
    up_pre = matmul(normed_rows_in, up_weights)
    hidden = (jax.nn.silu(gate_pre) * up_pre).astype(jnp.bfloat16)
    return (normed_rows_in, gate_pre, up_pre, hidden)


def gated_unit(gate_in, up_in):
    return jax.nn.silu(gate_in) * up_in


def local_tokens(
    layer_input,
    segment_ids,
    first_gain,
    query_down,
    query_gain,
    query_up,
    key_proj,
    value_proj,
    out_proj,
    second_gain,
    w_gate,
    w_up,
    w_down,
    cotangent,
):
    inputs = layer_input[0].astype(jnp.float32)
    segment_row = segment_ids[0]
    tok_rows = inputs.shape[0]
    positions = lax.axis_index("seq") * tok_rows + jnp.arange(tok_rows, dtype=jnp.int32)
    cosine_table, sine_table = angle_tables(positions, HEAD)
    weights_all = gather_layer(
        first_gain, query_down, query_gain, query_up, key_proj, value_proj, out_proj, second_gain
    )
    stored_front = front_pass(inputs, segment_row, weights_all, positions, cosine_table, sine_table)
    feed_state = feed_front(stored_front[8], w_gate, w_up)
    hidden_now = feed_state[3]
    branch_out = lax.psum_scatter(
        matmul(hidden_now, w_down), "seq", scatter_dimension=0, tiled=True
    )
    layer_out = stored_front[7] + branch_out
    weights_all = gather_layer(
        first_gain, query_down, query_gain, query_up, key_proj, value_proj, out_proj, second_gain
    )
    stored_front = front_pass(inputs, segment_row, weights_all, positions, cosine_table, sine_table)
    feed_state = feed_front(stored_front[8], w_gate, w_up)
    (
        gain_first,
        down_query,
        gain_query,
        up_query,
        key_weights,
        value_weights,
        out_weights,
        gain_second,
    ) = weights_all
    normed_in, query_low, query_norm, queries, kv_all, attention, attended, mid_sum, normed_mid = (
        stored_front
    )
    normed_all, gate_pre, up_pre, hidden = feed_state
    cot_rows = cotangent[0]
    piece_rows = lax.all_gather(cot_rows, "seq", axis=0, tiled=True)
    down_grad = dot_across(hidden, piece_rows)
    grad_hidden = dot_transposed(piece_rows, w_down)
    gated_value, gate_pull = jax.vjp(gated_unit, gate_pre, up_pre)
    gate_grad, up_grad = gate_pull(grad_hidden)
    gate_grad = gate_grad.astype(jnp.bfloat16)
    up_grad = up_grad.astype(jnp.bfloat16)
    gating_grad = dot_across(normed_all, gate_grad)
    upward_grad = dot_across(normed_all, up_grad)
    normed_grad = lax.psum_scatter(
        dot_transposed(gate_grad, w_gate) + dot_transposed(up_grad, w_up),
        "seq",
        scatter_dimension=0,
        tiled=True,
    )
    feed_grads = lax.psum((gating_grad, upward_grad, down_grad), "dp")
    norm_value, second_pull = jax.vjp(norm_apply, mid_sum, gain_second.astype(jnp.float32))
    mid_grad, second_grad = second_pull(normed_grad)
    mid_grad = mid_grad + cot_rows.astype(jnp.float32)
    attn_grad = mid_grad.astype(jnp.bfloat16)
    output_grad = dot_across(attended, attn_grad)
    context_grad = (
        dot_transposed(attn_grad, out_weights).astype(jnp.bfloat16).reshape(tok_rows, HEADS, HEAD)
    )
    key_all = kv_all[:, :HEAD]
    value_all = kv_all[:, HEAD:]
    scale_value = HEAD ** (-0.5)
    probs_grad = jnp.einsum(
        "thd,sd->ths", context_grad, value_all, preferred_element_type=jnp.float32
    )
    inner_sum = jnp.sum(attention * probs_grad, -1, keepdims=True)
    logit_grad = (attention * (probs_grad - inner_sum)).astype(jnp.bfloat16)
    queries_grad = (
        jnp.einsum("ths,sd->thd", logit_grad, key_all, preferred_element_type=jnp.float32)
        * scale_value
    )
    keys_grad = (
        jnp.einsum("ths,thd->sd", logit_grad, queries, preferred_element_type=jnp.float32)
        * scale_value
    )
    values_grad = jnp.einsum(
        "ths,thd->sd",
        attention.astype(jnp.bfloat16),
        context_grad,
        preferred_element_type=jnp.float32,
    )
    kv_grads = lax.psum_scatter(
        jnp.concatenate([keys_grad, values_grad], -1), "seq", scatter_dimension=0, tiled=True
    )
    key_grad = rotate(kv_grads[:, :HEAD], cosine_table, -sine_table).astype(jnp.bfloat16)
    value_grad = kv_grads[:, HEAD:].astype(jnp.bfloat16)
    query_grad = rotate(queries_grad, cosine_table[:, None, :], -sine_table[:, None, :])
    query_grad = query_grad.reshape(tok_rows, HEADS * HEAD).astype(jnp.bfloat16)
    lifted_grad = dot_across(query_norm, query_grad)
    compact_grad = dot_transposed(query_grad, up_query)
    query_value, query_pull = jax.vjp(norm_apply, query_low, gain_query.astype(jnp.float32))
    latent_grad, compact_gain = query_pull(compact_grad)
    latent_grad = latent_grad.astype(jnp.bfloat16)
    compress_grad = dot_across(normed_in, latent_grad)
    keymap_grad = dot_across(normed_in, key_grad)
    valuemap_grad = dot_across(normed_in, value_grad)
    entry_grad = (
        dot_transposed(latent_grad, down_query)
        + dot_transposed(key_grad, key_weights)
        + dot_transposed(value_grad, value_weights)
    )
    first_value, first_pull = jax.vjp(norm_apply, inputs, gain_first.astype(jnp.float32))
    inputs_grad, first_grad = first_pull(entry_grad)
    inputs_grad = inputs_grad + mid_grad
    layer_grads = (
        lax.psum_scatter(first_grad, ("dp", "seq"), scatter_dimension=0, tiled=True),
        lax.psum_scatter(compress_grad, ("dp", "seq"), scatter_dimension=0, tiled=True),
        lax.psum_scatter(compact_gain, ("dp", "seq"), scatter_dimension=0, tiled=True),
        lax.psum_scatter(lifted_grad, ("dp", "seq"), scatter_dimension=0, tiled=True),
        lax.psum_scatter(keymap_grad, ("dp", "seq"), scatter_dimension=0, tiled=True),
        lax.psum_scatter(valuemap_grad, ("dp", "seq"), scatter_dimension=0, tiled=True),
        lax.psum_scatter(output_grad, ("dp", "seq"), scatter_dimension=0, tiled=True),
        lax.psum_scatter(second_grad, ("dp", "seq"), scatter_dimension=0, tiled=True),
    )
    return (
        layer_out[None],
        inputs_grad[None],
        layer_grads[0],
        layer_grads[1],
        layer_grads[2],
        layer_grads[3],
        layer_grads[4],
        layer_grads[5],
        layer_grads[6],
        layer_grads[7],
        feed_grads[0],
        feed_grads[1],
        feed_grads[2],
    )


def tie(*values):
    return lax.optimization_barrier(values)


def gather_rows(block, row_count):
    row_at = lax.axis_index("dp")
    result = jnp.zeros((row_count,) + block.shape, block.dtype)
    result = lax.dynamic_update_index_in_dim(result, block, row_at, 0)
    for hop in range(1, row_count):
        moved = lax.ppermute(block, "dp", [(i, i ^ hop) for i in range(row_count)])
        result = lax.dynamic_update_index_in_dim(result, moved, row_at ^ hop, 0)
    return result


def sum_rows(blocks, row_count):
    row_at = lax.axis_index("dp")
    total = lax.dynamic_index_in_dim(blocks, row_at, 0, False).astype(jnp.float32)
    for hop in range(1, row_count):
        given = lax.dynamic_index_in_dim(blocks, row_at ^ hop, 0, False)
        moved = lax.ppermute(given, "dp", [(i, i ^ hop) for i in range(row_count)])
        total = total + moved.astype(jnp.float32)
    return total


def swap_rows(block, hop):
    return lax.ppermute(block, "dp", [(i, i ^ hop) for i in range(4)])


class SquareSum:
    def __init__(self, product, size, axis, first, second):
        row_at = lax.axis_index("dp")
        self.product, self.axis = product, axis
        self.first, self.second = first, second
        self.half, self.quarter = size // 2, size // 4
        self.upper_half = (row_at // first) % 2
        self.upper_quarter = (row_at // second) % 2

    def make(self, half, quarter):
        return self.product(half * self.half + quarter * self.quarter, self.quarter)

    def give(self, quarter):
        return self.make(1 - self.upper_half, quarter).astype(jnp.bfloat16)

    def give_passed(self):
        return self.give(1 - self.upper_quarter)

    def give_kept(self):
        return self.give(self.upper_quarter)

    def send(self, block):
        return swap_rows(block, self.first)

    def pass_on(self, moved):
        own = self.make(self.upper_half, 1 - self.upper_quarter)
        return swap_rows((own + moved.astype(jnp.float32)).astype(jnp.bfloat16), self.second)

    def finish(self, moved, passed):
        own = self.make(self.upper_half, self.upper_quarter)
        return (own + moved.astype(jnp.float32) + passed.astype(jnp.float32)).astype(
            jnp.bfloat16
        )

    def spread_once(self, own):
        return swap_rows(own, self.first), swap_rows(own, self.second)

    def spread_twice(self, beside):
        return swap_rows(beside, self.first)

    def assemble(self, result, base, own, across, beside, far):
        for block, half, quarter in (
            (own, self.upper_half, self.upper_quarter),
            (beside, self.upper_half, 1 - self.upper_quarter),
            (across, 1 - self.upper_half, self.upper_quarter),
            (far, 1 - self.upper_half, 1 - self.upper_quarter),
        ):
            start = base + half * self.half + quarter * self.quarter
            result = lax.dynamic_update_slice_in_dim(
                result, block.astype(jnp.float32), start, self.axis
            )
        return result


def turn(block, cosine, sine):
    half = block.shape[-1] // 2
    first, second = block[:, :half], block[:, half:]
    return jnp.concatenate([first * cosine - second * sine, second * cosine + first * sine], -1)


def kv_block(kv_ref, at):
    rows = kv_ref.shape[1] // 2
    return jnp.concatenate([kv_ref[at, :rows], kv_ref[at, rows:]], -1)


def low_block(low_ref, gain_ref):
    low = jnp.concatenate([low_ref[i] for i in range(low_ref.shape[0])], -1).astype(jnp.float32)
    gain = jnp.concatenate([gain_ref[i : i + 1] for i in range(gain_ref.shape[0])], -1)
    scale = lax.rsqrt(jnp.mean(low * low, -1, keepdims=True) + epsilon)
    return low * scale, gain


def block_weights(query, kv_ref, seg_query_ref, seg_key_ref, step, parts):
    rows = query.shape[0]
    keys = jnp.concatenate([kv_block(kv_ref, j) for j in range(step + 1)], 0)
    logits = dot_transposed(query, keys) * query.shape[1] ** (-0.5)
    count = (step + 1) * rows
    row_at = step * rows + lax.broadcasted_iota(jnp.int32, (rows, count), 0)
    col_at = lax.broadcasted_iota(jnp.int32, (rows, count), 1)
    allowed = (col_at <= row_at) & (seg_query_ref[...] == seg_key_ref[:, :count])
    logits = jnp.where(allowed, logits, masked_value)
    powers = jnp.exp(logits - jnp.max(logits, -1, keepdims=True))
    return powers / jnp.sum(powers, -1, keepdims=True), keys


def attend_kernel(
    parts,
    low_ref,
    kv_ref,
    gain_ref,
    cosine_ref,
    sine_ref,
    seg_query_ref,
    seg_key_ref,
    up_ref,
    out_ref,
    mixed_ref,
    queries_ref,
    attended_ref,
    norm_ref,
):
    def block(step):
        unit, gain = low_block(low_ref, gain_ref)
        query_norm = (unit * gain).astype(jnp.bfloat16)
        norm_ref[...] = query_norm
        raw = matmul(query_norm, up_ref[...])
        values = jnp.concatenate([kv_block(kv_ref, parts + j) for j in range(step + 1)], 0)
        for head in range(raw.shape[1] // HEAD):
            cols = slice(head * HEAD, (head + 1) * HEAD)
            query = turn(raw[:, cols], cosine_ref[...], sine_ref[...]).astype(jnp.bfloat16)
            queries_ref[:, cols] = query
            weights, _ = block_weights(query, kv_ref, seg_query_ref, seg_key_ref, step, parts)
            attended_ref[:, cols] = matmul(weights.astype(jnp.bfloat16), values).astype(
                jnp.bfloat16
            )
        mixed_ref[...] = matmul(attended_ref[...], out_ref[...]).astype(jnp.bfloat16)

    for step in range(parts):
        pl.when(pl.program_id(0) == step)(functools.partial(block, step))


def attend_back_kernel(
    parts,
    grad_ref,
    queries_ref,
    low_ref,
    kv_ref,
    gain_ref,
    cosine_ref,
    sine_ref,
    seg_query_ref,
    seg_key_ref,
    up_ref,
    out_ref,
    back_ref,
    query_grad_ref,
    keys_sum,
    values_sum,
    means,
):
    slots = low_ref.shape[0]
    lanes = low_ref.shape[2]

    def block(step):
        unit, gain = low_block(low_ref, gain_ref)
        rows = unit.shape[0]
        scale_value = HEAD ** (-0.5)
        context = dot_transposed(grad_ref[...], out_ref[...]).astype(jnp.bfloat16)
        values = jnp.concatenate([kv_block(kv_ref, parts + j) for j in range(step + 1)], 0)
        count = (step + 1) * rows
        last = slice(step * rows, count)
        keys_sum[last] = jnp.zeros((rows, HEAD), jnp.float32)
        values_sum[last] = jnp.zeros((rows, HEAD), jnp.float32)
        for head in range(context.shape[1] // HEAD):
            cols = slice(head * HEAD, (head + 1) * HEAD)
            query = queries_ref[:, cols]
            weights, keys = block_weights(query, kv_ref, seg_query_ref, seg_key_ref, step, parts)
            probs = dot_transposed(context[:, cols], values)
            inner = jnp.sum(weights * probs, -1, keepdims=True)
            logit_grad = (weights * (probs - inner)).astype(jnp.bfloat16)
            turned = matmul(logit_grad, keys) * scale_value
            query_grad_ref[:, cols] = turn(turned, cosine_ref[...], -sine_ref[...]).astype(
                jnp.bfloat16
            )
            keys_sum[:count] += dot_across(logit_grad, query) * scale_value
            values_sum[:count] += dot_across(weights.astype(jnp.bfloat16), context[:, cols])
        compact = dot_transposed(query_grad_ref[...], up_ref[...])
        for slot in range(slots):
            back_ref[slot, last] = compact[:, slot * lanes : (slot + 1) * lanes].astype(
                jnp.bfloat16
            )
        mean = jnp.sum(compact * gain * unit, -1, keepdims=True) / compact.shape[1]
        mean = jnp.broadcast_to(mean, (rows, lanes)).T
        for part in range(rows // lanes):
            at = step * (rows // lanes) + part
            means[at : at + 1] = mean[:1, part * lanes : (part + 1) * lanes]
        if step == parts - 1:
            length = parts * rows
            mean_high = means[...].astype(jnp.bfloat16)
            mean_low = (means[...] - mean_high.astype(jnp.float32)).astype(jnp.bfloat16)
            tail = length + 2 * rows
            size = means.shape[0]
            for slot in range(slots):
                total = keys_sum if slot < parts else values_sum
                own = total[(slot % parts) * rows : (slot % parts + 1) * rows].astype(jnp.bfloat16)
                back_ref[slot, length : length + rows] = own[:, :lanes]
                back_ref[slot, length + rows : tail] = own[:, lanes:]
                back_ref[slot, tail : tail + size] = mean_high
                back_ref[slot, tail + size : tail + 2 * size] = mean_low

    for step in range(parts):
        pl.when(pl.program_id(0) == step)(functools.partial(block, step))


def attention_specs(parts, slots, length, lanes, low_width, head_width, width):
    rows = length // parts
    return [
        pl.BlockSpec((slots, rows, lanes), lambda i: (0, i, 0)),
        pl.BlockSpec((slots, 2 * rows, lanes), lambda i: (0, length // (2 * rows), 0)),
        pl.BlockSpec((slots, lanes), lambda i: (0, 0)),
        pl.BlockSpec((rows, HEAD // 2), lambda i: (i, 0)),
        pl.BlockSpec((rows, HEAD // 2), lambda i: (i, 0)),
        pl.BlockSpec((rows, 1), lambda i: (i, 0)),
        pl.BlockSpec((1, length), lambda i: (0, 0)),
        pl.BlockSpec((low_width, head_width), lambda i: (0, 0)),
        pl.BlockSpec((head_width, width), lambda i: (0, 0)),
    ]


def attend(parts, low_all, gain, cosine, sine, segment_row, up_mine, out_mine):
    slots, _, lanes = low_all.shape
    length = segment_row.shape[0]
    low_width, head_width = up_mine.shape
    width = out_mine.shape[1]
    rows = length // parts
    bf16 = jnp.bfloat16
    return pl.pallas_call(
        functools.partial(attend_kernel, parts),
        grid=(parts,),
        in_specs=attention_specs(parts, slots, length, lanes, low_width, head_width, width),
        out_specs=[
            pl.BlockSpec((rows, width), lambda i: (i, 0)),
            pl.BlockSpec((rows, head_width), lambda i: (i, 0)),
            pl.BlockSpec((rows, head_width), lambda i: (i, 0)),
            pl.BlockSpec((rows, low_width), lambda i: (i, 0)),
        ],
        out_shape=[
            jax.ShapeDtypeStruct((length, width), bf16),
            jax.ShapeDtypeStruct((length, head_width), bf16),
            jax.ShapeDtypeStruct((length, head_width), bf16),
            jax.ShapeDtypeStruct((length, low_width), bf16),
        ],
        compiler_params=pltpu.CompilerParams(vmem_limit_bytes=48 * 1024 * 1024),
        cost_estimate=pl.CostEstimate(
            flops=8 * 10**9, bytes_accessed=16 * 10**6, transcendentals=2 * 10**6
        ),
        name="attend",
    )(
        low_all,
        low_all,
        gain,
        cosine,
        sine,
        segment_row[:, None],
        segment_row[None],
        up_mine,
        out_mine,
    )


def attend_back(
    parts, grad, queries, low_all, gain, cosine, sine, segment_row, up_mine, out_mine
):
    slots, _, lanes = low_all.shape
    length = segment_row.shape[0]
    low_width, head_width = up_mine.shape
    width = out_mine.shape[1]
    rows = length // parts
    means = length // lanes
    total = length + 2 * rows + 2 * means
    bf16 = jnp.bfloat16
    return pl.pallas_call(
        functools.partial(attend_back_kernel, parts),
        grid=(parts,),
        in_specs=[
            pl.BlockSpec((rows, width), lambda i: (i, 0)),
            pl.BlockSpec((rows, head_width), lambda i: (i, 0)),
        ]
        + attention_specs(parts, slots, length, lanes, low_width, head_width, width),
        out_specs=[
            pl.BlockSpec((slots, total, lanes), lambda i: (0, 0, 0)),
            pl.BlockSpec((rows, head_width), lambda i: (i, 0)),
        ],
        out_shape=[
            jax.ShapeDtypeStruct((slots, total, lanes), bf16),
            jax.ShapeDtypeStruct((length, head_width), bf16),
        ],
        scratch_shapes=[
            pltpu.VMEM((length, HEAD), jnp.float32),
            pltpu.VMEM((length, HEAD), jnp.float32),
            pltpu.VMEM((means, lanes), jnp.float32),
        ],
        compiler_params=pltpu.CompilerParams(vmem_limit_bytes=48 * 1024 * 1024),
        cost_estimate=pl.CostEstimate(
            flops=12 * 10**9, bytes_accessed=20 * 10**6, transcendentals=2 * 10**6
        ),
        name="attend_back",
    )(
        grad,
        queries,
        low_all,
        low_all,
        gain,
        cosine,
        sine,
        segment_row[:, None],
        segment_row[None],
        up_mine,
        out_mine,
    )


def local_heads(
    row_count,
    seq_count,
    layer_input,
    segment_ids,
    first_gain,
    query_down,
    query_gain,
    query_up,
    key_proj,
    value_proj,
    out_proj,
    second_gain,
    w_gate,
    w_up,
    w_down,
    cotangent,
):
    f32, bf16 = jnp.float32, jnp.bfloat16
    seq_at = lax.axis_index("seq")
    core_at = lax.rem(seq_at, 2)
    swap = [(i, i ^ 1) for i in range(seq_count)]
    own_rows = layer_input.shape[1]
    length = own_rows * seq_count
    width = layer_input.shape[2]
    low_width = query_down.shape[1]
    down_rows = query_down.shape[0]
    up_rows = query_up.shape[0]
    out_rows = out_proj.shape[0]
    half_count = row_count // 2
    chips = seq_count // 2
    own_low = low_width // seq_count
    low_part = own_low // row_count
    kv_parts = seq_count // 2
    kv_rows = length // kv_parts
    kv_at = lax.rem(seq_at, kv_parts)
    is_key = seq_at < kv_parts
    spare = 8
    own_heads = half_count

    gains = jnp.zeros((spare, own_low + HEAD), bf16)
    gains = gains.at[0, :down_rows].set(first_gain)
    gains = gains.at[1, :down_rows].set(second_gain)
    gains = gains.at[2, :up_rows].set(query_gain)
    low_cols = query_down.reshape(down_rows, row_count, seq_count, low_part)
    low_cols = low_cols.transpose(2, 0, 1, 3).reshape(seq_count, down_rows, own_low)
    kv_cols = jnp.stack([key_proj] * kv_parts + [value_proj] * kv_parts)
    sent = jnp.concatenate([low_cols, kv_cols], -1)
    sent = jnp.concatenate(
        [sent, jnp.broadcast_to(gains[None], (seq_count, spare, own_low + HEAD))], 1
    )
    sent = sent.reshape(seq_count * (down_rows + spare), own_low + HEAD)
    sent = lax.all_to_all(sent, "seq", 0, 0, tiled=True)
    entry_all = gather_rows(sent, row_count)
    entry_all = entry_all.reshape(row_count * seq_count, down_rows + spare, own_low + HEAD)
    entry_weights = entry_all[:, :down_rows].reshape(width, own_low + HEAD)
    gain_first = entry_all[:, down_rows, :down_rows].reshape(width).astype(f32)
    gain_second = entry_all[:, down_rows + 1, :down_rows].reshape(width).astype(f32)
    gain_query = entry_all[:, down_rows + 2, :up_rows].reshape(row_count, seq_count, low_part)
    gain_query = gain_query.transpose(1, 0, 2).reshape(low_width).astype(f32)

    inputs_all = lax.all_gather(layer_input[0], "seq", axis=0, tiled=True)

    up_sent = query_up.reshape(up_rows, 2, half_count, chips, HEAD).transpose(3, 1, 0, 2, 4)
    up_sent = up_sent.reshape(seq_count * up_rows, own_heads * HEAD)
    up_mine = lax.all_to_all(up_sent, "seq", 0, 0, tiled=True)
    up_mine = gather_rows(up_mine, row_count)
    up_mine = up_mine.reshape(row_count, seq_count, low_part, own_heads * HEAD)
    up_mine = up_mine.transpose(1, 0, 2, 3).reshape(low_width, own_heads * HEAD)

    out_all = gather_rows(out_proj, row_count)
    out_kept = lax.dynamic_slice_in_dim(out_all, core_at * half_count, half_count, 0)
    out_given = lax.dynamic_slice_in_dim(out_all, (1 - core_at) * half_count, half_count, 0)
    out_got = lax.ppermute(out_given, "seq", swap)
    out_mine = jnp.where(
        core_at == 0,
        jnp.stack([out_kept, out_got], 1),
        jnp.stack([out_got, out_kept], 1),
    ).reshape(own_heads * HEAD, width)

    cot_rows = cotangent[0]
    cot_all = lax.all_gather(cot_rows, "seq", axis=0, tiled=True)

    positions = jnp.arange(length, dtype=jnp.int32)
    cosine_table, sine_table = angle_tables(positions, HEAD)

    inputs_wide = inputs_all.astype(f32)
    entry_scale = lax.rsqrt(jnp.mean(inputs_wide * inputs_wide, -1, keepdims=True) + epsilon)
    normed_in = (inputs_wide * entry_scale * gain_first).astype(bf16)
    low_own = matmul(normed_in, entry_weights)
    kv_own = lax.dynamic_slice_in_dim(low_own[:, own_low:], kv_at * kv_rows, kv_rows, 0)
    kv_cos = lax.dynamic_slice_in_dim(cosine_table, kv_at * kv_rows, kv_rows, 0)
    kv_sin = lax.dynamic_slice_in_dim(sine_table, kv_at * kv_rows, kv_rows, 0)
    kv_own = jnp.where(is_key, rotate(kv_own, kv_cos, kv_sin), kv_own).astype(bf16)
    half_head = HEAD // 2
    low_sent = jnp.concatenate(
        [low_own[:, :own_low].astype(bf16), kv_own[:, :half_head], kv_own[:, half_head:]], 0
    )
    low_all = lax.all_gather(low_sent, "seq", axis=0, tiled=False)

    segment_row = segment_ids[0]
    gain_slots = gain_query.reshape(seq_count, own_low)
    half_cos, half_sin = cosine_table[:, :half_head], sine_table[:, :half_head]
    mixed, queries, attended, query_norm = attend(
        kv_parts, low_all, gain_slots, half_cos, half_sin, segment_row, up_mine, out_mine
    )
    mixed = lax.psum_scatter(mixed, "seq", scatter_dimension=0, tiled=True).astype(f32)
    mid_sum = layer_input[0].astype(f32) + mixed
    mid_scale = lax.rsqrt(jnp.mean(mid_sum * mid_sum, -1, keepdims=True) + epsilon)
    mid_unit = mid_sum * mid_scale
    normed_mid = (mid_unit * gain_second).astype(bf16)

    grad_hidden = dot_transposed(cot_all, w_down)
    normed_mid, grad_hidden = tie(normed_mid, grad_hidden)
    normed_all = lax.all_gather(normed_mid, "seq", axis=0, tiled=True)
    gate_pre = matmul(normed_all, w_gate)
    up_pre = matmul(normed_all, w_up)
    hidden = gated_unit(gate_pre, up_pre)
    gated_value, gate_pull = jax.vjp(gated_unit, gate_pre, up_pre)
    hidden = gated_value.astype(bf16)
    gate_grad, up_grad = gate_pull(grad_hidden)
    gate_grad = gate_grad.astype(bf16)
    up_grad = up_grad.astype(bf16)
    normed_grad = dot_transposed(gate_grad, w_gate) + dot_transposed(up_grad, w_up)
    normed_grad = lax.psum_scatter(
        normed_grad.astype(bf16), "seq", scatter_dimension=0, tiled=True
    ).astype(f32)
    def from_columns(left, right):
        return lambda start, size: dot_across(
            lax.dynamic_slice_in_dim(left, start, size, 1), right
        )

    def to_columns(left, right, base):
        return lambda start, size: dot_across(
            left, lax.dynamic_slice_in_dim(right, base + start, size, 1)
        )

    half_width = width // 2
    sums = [
        SquareSum(from_columns(normed_all, gate_grad), width, 0, 1, 2),
        SquareSum(from_columns(normed_all, up_grad), width, 0, 2, 1),
        SquareSum(to_columns(hidden, cot_all, 0), half_width, 1, 1, 2),
        SquareSum(to_columns(hidden, cot_all, half_width), half_width, 1, 2, 1),
    ]
    passed = [one.send(one.give_passed()) for one in sums]
    kept = [one.give_kept() for one in sums]
    hidden_out = matmul(hidden, w_down).astype(bf16)
    moved = [one.send(block) for one, block in zip(sums[2:], kept[2:])]
    normed_grad, kept[0], kept[1], hidden_out, moved, passed = tie(
        normed_grad, kept[0], kept[1], hidden_out, moved, passed
    )
    moved = [one.send(block) for one, block in zip(sums[:2], kept[:2])] + moved
    passed = [one.pass_on(block) for one, block in zip(sums, passed)]

    second_grad = jnp.sum(normed_grad * mid_unit, 0)
    scaled_grad = normed_grad * gain_second
    mid_grad = mid_scale * (
        scaled_grad - mid_unit * jnp.mean(scaled_grad * mid_unit, -1, keepdims=True)
    )
    mid_grad = mid_grad + cot_rows.astype(f32)
    attn_grad = lax.all_gather(mid_grad.astype(bf16), "seq", axis=0, tiled=True)

    attn_grad, moved, passed, hidden_out = tie(attn_grad, moved, passed, hidden_out)
    branch_out = lax.psum_scatter(hidden_out, "seq", scatter_dimension=0, tiled=True)
    back_sent, query_grad = attend_back(
        kv_parts,
        attn_grad,
        queries,
        low_all,
        gain_slots,
        half_cos,
        half_sin,
        segment_row,
        up_mine,
        out_mine,
    )
    output_grad = dot_across(attended, attn_grad).astype(bf16)
    output_grad = output_grad.reshape(own_heads, 2, out_rows, width)
    grad_kept = lax.dynamic_index_in_dim(output_grad, core_at, 1, False)
    grad_given = lax.dynamic_index_in_dim(output_grad, 1 - core_at, 1, False)
    grad_got = lax.ppermute(grad_given, "seq", swap)
    output_grad = jnp.where(
        core_at == 0,
        jnp.concatenate([grad_kept, grad_got], 0),
        jnp.concatenate([grad_got, grad_kept], 0),
    )
    output_grad = sum_rows(output_grad, row_count)
    owned = [one.finish(block, more) for one, block, more in zip(sums, moved, passed)]
    spread = [one.spread_once(block) for one, block in zip(sums[2:], owned[2:])]
    back_sent, branch_out, output_grad, owned[0], owned[1], spread = tie(
        back_sent, branch_out, output_grad, owned[0], owned[1], spread
    )
    spread = [one.spread_once(block) for one, block in zip(sums[:2], owned[:2])] + spread
    back = lax.psum_scatter(back_sent, "seq", scatter_dimension=0, tiled=False).astype(f32)

    lifted_grad = dot_across(query_norm, query_grad).astype(bf16)
    back, lifted_grad, spread = tie(back, lifted_grad, spread)

    compact_own = back[:length]
    kv_back = jnp.concatenate(
        [back[length : length + kv_rows], back[length + kv_rows : length + 2 * kv_rows]], -1
    )
    mean_back = back[length + 2 * kv_rows :].reshape(2, length).sum(0)[:, None]
    low_at = seq_at * own_low
    query_low = low_all[:, :length].astype(f32)
    query_scale = jnp.sum(query_low * query_low, (0, 2)) / low_width
    query_scale = lax.rsqrt(query_scale + epsilon)[:, None]
    low_mine = lax.dynamic_index_in_dim(low_all, seq_at, 0, False)[:length].astype(f32)
    unit_own = low_mine * query_scale
    gain_own = lax.dynamic_slice_in_dim(gain_query, low_at, own_low, 0)
    compact_gain = jnp.sum(compact_own * unit_own, 0)
    latent_grad = (query_scale * (compact_own * gain_own - unit_own * mean_back)).astype(bf16)
    kv_back = jnp.where(is_key, rotate(kv_back, kv_cos, -kv_sin), kv_back).astype(bf16)
    kv_padded = lax.dynamic_update_slice_in_dim(
        jnp.zeros((length, HEAD), bf16), kv_back, kv_at * kv_rows, 0
    )
    entry_sent = jnp.concatenate([latent_grad, kv_padded], -1)
    entry_part = dot_transposed(entry_sent, entry_weights)
    blocks_of = [
        (own, across, beside, one.spread_twice(beside))
        for one, own, (across, beside) in zip(sums, owned, spread)
    ]
    units = w_gate.shape[1]
    gating_grad = sums[0].assemble(jnp.zeros((width, units), f32), 0, *blocks_of[0])
    upward_grad = sums[1].assemble(jnp.zeros((width, units), f32), 0, *blocks_of[1])
    down_grad = sums[2].assemble(jnp.zeros((units, width), f32), 0, *blocks_of[2])
    down_grad = sums[3].assemble(down_grad, half_width, *blocks_of[3])
    lifted_grad = lifted_grad.reshape(seq_count, row_count, up_rows, own_heads * HEAD)
    lifted_grad = lifted_grad.transpose(1, 0, 2, 3)
    lifted_grad = lifted_grad.reshape(row_count, seq_count * up_rows, own_heads * HEAD)
    lifted_grad = sum_rows(lifted_grad, row_count).astype(bf16)
    entry_grad = lax.psum_scatter(
        entry_part.astype(bf16), "seq", scatter_dimension=0, tiled=True
    ).astype(f32)
    first_grad = jnp.sum(entry_part * (inputs_wide * entry_scale), 0)
    blocks = row_count * seq_count
    weight_grad = dot_across(normed_in, entry_sent).astype(bf16)
    weight_grad = weight_grad.reshape(blocks, down_rows, own_low + HEAD)
    mine = (jnp.arange(seq_count) == seq_at)[None, :, None]
    gain_back = jnp.where(mine, compact_gain.reshape(row_count, 1, low_part), 0.0)
    extra = jnp.zeros((blocks, spare, own_low + HEAD), f32)
    extra = extra.at[:, 0, :down_rows].set(first_grad.reshape(blocks, down_rows))
    extra = extra.at[:, 1, :down_rows].set(second_grad.reshape(blocks, down_rows))
    extra = extra.at[:, 2, :low_part].set(gain_back.reshape(blocks, low_part))
    weight_grad = jnp.concatenate([weight_grad, extra.astype(bf16)], 1)
    weight_grad = weight_grad.reshape(
        row_count, seq_count * (down_rows + spare), own_low + HEAD
    )
    weight_grad = sum_rows(weight_grad, row_count).astype(bf16)
    weight_grad = lax.all_to_all(weight_grad, "seq", 0, 0, tiled=True).astype(f32)
    weight_grad = weight_grad.reshape(seq_count, down_rows + spare, own_low + HEAD)
    compress_grad = weight_grad[:, :down_rows, :own_low].reshape(
        seq_count, down_rows, row_count, low_part
    )
    compress_grad = compress_grad.transpose(1, 2, 0, 3).reshape(down_rows, low_width)
    keymap_grad = jnp.sum(weight_grad[:kv_parts, :down_rows, own_low:], 0)
    valuemap_grad = jnp.sum(weight_grad[kv_parts:, :down_rows, own_low:], 0)
    gain_rows = jnp.sum(weight_grad[:, down_rows:], 0)
    lifted_grad = lax.all_to_all(lifted_grad, "seq", 0, 0, tiled=True)
    lifted_grad = lifted_grad.reshape(chips, 2, up_rows, half_count, HEAD)
    lifted_grad = lifted_grad.transpose(2, 1, 3, 0, 4).reshape(up_rows, HEADS * HEAD)

    entry_grad, compress_grad, lifted_grad, output_grad, spread = tie(
        entry_grad, compress_grad, lifted_grad, output_grad, spread
    )
    layer_out = mid_sum + branch_out.astype(f32)
    own_at = seq_at * own_rows
    inputs_own = layer_input[0].astype(f32)
    scale_own = lax.dynamic_slice_in_dim(entry_scale, own_at, own_rows, 0)
    entry_unit = inputs_own * scale_own
    entry_scaled = entry_grad * gain_first
    inputs_grad = scale_own * (
        entry_scaled - entry_unit * jnp.mean(entry_scaled * entry_unit, -1, keepdims=True)
    )
    inputs_grad = inputs_grad + mid_grad

    return (
        layer_out[None],
        inputs_grad[None],
        gain_rows[0, :down_rows],
        compress_grad,
        gain_rows[2, :low_part],
        lifted_grad.astype(f32),
        keymap_grad,
        valuemap_grad,
        output_grad.astype(f32),
        gain_rows[1, :down_rows],
        gating_grad,
        upward_grad,
        down_grad,
    )


def solution(mesh):
    row_count, seq_count = mesh.shape["dp"], mesh.shape["seq"]
    if row_count == 4 and seq_count % 2 == 0 and HEADS * 2 == row_count * seq_count:
        local = functools.partial(local_heads, row_count, seq_count)
    else:
        local = local_tokens
    return jax.shard_map(
        local,
        mesh=mesh,
        in_specs=(
            P("dp", "seq", None),
            P("dp", None),
            P(("dp", "seq")),
            P(("dp", "seq"), None),
            P(("dp", "seq")),
            P(("dp", "seq"), None),
            P(("dp", "seq"), None),
            P(("dp", "seq"), None),
            P(("dp", "seq"), None),
            P(("dp", "seq")),
            P(None, "seq"),
            P(None, "seq"),
            P("seq", None),
            P("dp", "seq", None),
        ),
        out_specs=(
            P("dp", "seq", None),
            P("dp", "seq", None),
            P(("dp", "seq")),
            P(("dp", "seq"), None),
            P(("dp", "seq")),
            P(("dp", "seq"), None),
            P(("dp", "seq"), None),
            P(("dp", "seq"), None),
            P(("dp", "seq"), None),
            P(("dp", "seq")),
            P(None, "seq"),
            P(None, "seq"),
            P("seq", None),
        ),
        check_vma=False,
    )
```

```python
import functools

import jax
import jax.numpy as jnp
from jax import lax
from jax.experimental import pallas as pl
from jax.experimental.pallas import tpu as pltpu
from jax.sharding import PartitionSpec as P

HEADS = 16
HEAD = 256


epsilon = 1e-06
masked_value = -1e30


def norm_apply(data_rows, gain_vec):
    inverse_rms = lax.rsqrt(jnp.mean(data_rows * data_rows, -1, keepdims=True) + epsilon)
    return data_rows * inverse_rms * gain_vec


def rotate(data_rows, cosine_table, sine_table):
    half_size = data_rows.shape[-1] // 2
    turned = jnp.concatenate([-data_rows[..., half_size:], data_rows[..., :half_size]], -1)
    return data_rows * cosine_table + turned * sine_table


def angle_tables(positions, head_size):
    frequency = 10000.0 ** (-jnp.arange(0, head_size, 2).astype(jnp.float32) / head_size)
    angles = positions.astype(jnp.float32)[:, None] * frequency[None, :]
    angles = jnp.concatenate([angles, angles], -1)
    return (jnp.cos(angles), jnp.sin(angles))


def matmul(left_op, right_op):
    return jnp.dot(left_op, right_op, preferred_element_type=jnp.float32)


def dot_across(left_op, right_op):
    return lax.dot_general(
        left_op, right_op, (((0,), (0,)), ((), ())), preferred_element_type=jnp.float32
    )


def dot_transposed(left_op, right_op):
    return lax.dot_general(
        left_op, right_op, (((1,), (1,)), ((), ())), preferred_element_type=jnp.float32
    )


def gather_layer(
    first_gain, query_down, query_gain, query_up, key_proj, value_proj, out_proj, second_gain
):
    return (
        lax.all_gather(first_gain, ("dp", "seq"), axis=0, tiled=True),
        lax.all_gather(query_down, ("dp", "seq"), axis=0, tiled=True),
        lax.all_gather(query_gain, ("dp", "seq"), axis=0, tiled=True),
        lax.all_gather(query_up, ("dp", "seq"), axis=0, tiled=True),
        lax.all_gather(key_proj, ("dp", "seq"), axis=0, tiled=True),
        lax.all_gather(value_proj, ("dp", "seq"), axis=0, tiled=True),
        lax.all_gather(out_proj, ("dp", "seq"), axis=0, tiled=True),
        lax.all_gather(second_gain, ("dp", "seq"), axis=0, tiled=True),
    )


def front_pass(inputs, segment_row, weights_all, positions, cosine_table, sine_table):
    (
        gain_first,
        down_query,
        gain_query,
        up_query,
        key_weights,
        value_weights,
        out_weights,
        gain_second,
    ) = weights_all
    tok_rows = inputs.shape[0]
    normed_in = norm_apply(inputs, gain_first.astype(jnp.float32)).astype(jnp.bfloat16)
    query_low = matmul(normed_in, down_query)
    query_norm = norm_apply(query_low, gain_query.astype(jnp.float32)).astype(jnp.bfloat16)
    query_raw = matmul(query_norm, up_query).reshape(tok_rows, HEADS, HEAD)
    queries = rotate(query_raw, cosine_table[:, None, :], sine_table[:, None, :]).astype(
        jnp.bfloat16
    )
    key_own = rotate(matmul(normed_in, key_weights), cosine_table, sine_table).astype(jnp.bfloat16)
    value_own = matmul(normed_in, value_weights).astype(jnp.bfloat16)
    key_value = jnp.concatenate([key_own, value_own], -1)
    kv_all = lax.all_gather(key_value, "seq", axis=0, tiled=True)
    own_segments = lax.dynamic_slice_in_dim(segment_row, positions[0], tok_rows, 0)
    all_positions = jnp.arange(segment_row.shape[0], dtype=jnp.int32)
    allowed = (all_positions[None, :] <= positions[:, None]) & (
        segment_row[None, :] == own_segments[:, None]
    )
    logits = jnp.einsum(
        "thd,sd->ths", queries, kv_all[:, :HEAD], preferred_element_type=jnp.float32
    ) * HEAD ** (-0.5)
    masked = jnp.where(allowed[:, None, :], logits, masked_value)
    attention = jax.nn.softmax(masked, axis=-1)
    attended = jnp.einsum(
        "ths,sd->thd",
        attention.astype(jnp.bfloat16),
        kv_all[:, HEAD:],
        preferred_element_type=jnp.float32,
    )
    attended = attended.reshape(tok_rows, HEADS * HEAD).astype(jnp.bfloat16)
    mid_sum = inputs + matmul(attended, out_weights)
    normed_mid = norm_apply(mid_sum, gain_second.astype(jnp.float32)).astype(jnp.bfloat16)
    return (
        normed_in,
        query_low,
        query_norm,
        queries,
        kv_all,
        attention,
        attended,
        mid_sum,
        normed_mid,
    )


def feed_front(normed_mid, w_gate, w_up):
    normed_all = lax.all_gather(normed_mid, "seq", axis=0, tiled=True)
    return feed_local(normed_all, w_gate, w_up)


def feed_local(normed_rows_in, gate_weights, up_weights):
    gate_pre = matmul(normed_rows_in, gate_weights)
    up_pre = matmul(normed_rows_in, up_weights)
    hidden = (jax.nn.silu(gate_pre) * up_pre).astype(jnp.bfloat16)
    return (normed_rows_in, gate_pre, up_pre, hidden)


def gated_unit(gate_in, up_in):
    return jax.nn.silu(gate_in) * up_in


def local_tokens(
    layer_input,
    segment_ids,
    first_gain,
    query_down,
    query_gain,
    query_up,
    key_proj,
    value_proj,
    out_proj,
    second_gain,
    w_gate,
    w_up,
    w_down,
    cotangent,
):
    inputs = layer_input[0].astype(jnp.float32)
    segment_row = segment_ids[0]
    tok_rows = inputs.shape[0]
    positions = lax.axis_index("seq") * tok_rows + jnp.arange(tok_rows, dtype=jnp.int32)
    cosine_table, sine_table = angle_tables(positions, HEAD)
    weights_all = gather_layer(
        first_gain, query_down, query_gain, query_up, key_proj, value_proj, out_proj, second_gain
    )
    stored_front = front_pass(inputs, segment_row, weights_all, positions, cosine_table, sine_table)
    feed_state = feed_front(stored_front[8], w_gate, w_up)
    hidden_now = feed_state[3]
    branch_out = lax.psum_scatter(
        matmul(hidden_now, w_down), "seq", scatter_dimension=0, tiled=True
    )
    layer_out = stored_front[7] + branch_out
    weights_all = gather_layer(
        first_gain, query_down, query_gain, query_up, key_proj, value_proj, out_proj, second_gain
    )
    stored_front = front_pass(inputs, segment_row, weights_all, positions, cosine_table, sine_table)
    feed_state = feed_front(stored_front[8], w_gate, w_up)
    (
        gain_first,
        down_query,
        gain_query,
        up_query,
        key_weights,
        value_weights,
        out_weights,
        gain_second,
    ) = weights_all
    normed_in, query_low, query_norm, queries, kv_all, attention, attended, mid_sum, normed_mid = (
        stored_front
    )
    normed_all, gate_pre, up_pre, hidden = feed_state
    cot_rows = cotangent[0]
    piece_rows = lax.all_gather(cot_rows, "seq", axis=0, tiled=True)
    down_grad = dot_across(hidden, piece_rows)
    grad_hidden = dot_transposed(piece_rows, w_down)
    gated_value, gate_pull = jax.vjp(gated_unit, gate_pre, up_pre)
    gate_grad, up_grad = gate_pull(grad_hidden)
    gate_grad = gate_grad.astype(jnp.bfloat16)
    up_grad = up_grad.astype(jnp.bfloat16)
    gating_grad = dot_across(normed_all, gate_grad)
    upward_grad = dot_across(normed_all, up_grad)
    normed_grad = lax.psum_scatter(
        dot_transposed(gate_grad, w_gate) + dot_transposed(up_grad, w_up),
        "seq",
        scatter_dimension=0,
        tiled=True,
    )
    feed_grads = lax.psum((gating_grad, upward_grad, down_grad), "dp")
    norm_value, second_pull = jax.vjp(norm_apply, mid_sum, gain_second.astype(jnp.float32))
    mid_grad, second_grad = second_pull(normed_grad)
    mid_grad = mid_grad + cot_rows.astype(jnp.float32)
    attn_grad = mid_grad.astype(jnp.bfloat16)
    output_grad = dot_across(attended, attn_grad)
    context_grad = (
        dot_transposed(attn_grad, out_weights).astype(jnp.bfloat16).reshape(tok_rows, HEADS, HEAD)
    )
    key_all = kv_all[:, :HEAD]
    value_all = kv_all[:, HEAD:]
    scale_value = HEAD ** (-0.5)
    probs_grad = jnp.einsum(
        "thd,sd->ths", context_grad, value_all, preferred_element_type=jnp.float32
    )
    inner_sum = jnp.sum(attention * probs_grad, -1, keepdims=True)
    logit_grad = (attention * (probs_grad - inner_sum)).astype(jnp.bfloat16)
    queries_grad = (
        jnp.einsum("ths,sd->thd", logit_grad, key_all, preferred_element_type=jnp.float32)
        * scale_value
    )
    keys_grad = (
        jnp.einsum("ths,thd->sd", logit_grad, queries, preferred_element_type=jnp.float32)
        * scale_value
    )
    values_grad = jnp.einsum(
        "ths,thd->sd",
        attention.astype(jnp.bfloat16),
        context_grad,
        preferred_element_type=jnp.float32,
    )
    kv_grads = lax.psum_scatter(
        jnp.concatenate([keys_grad, values_grad], -1), "seq", scatter_dimension=0, tiled=True
    )
    key_grad = rotate(kv_grads[:, :HEAD], cosine_table, -sine_table).astype(jnp.bfloat16)
    value_grad = kv_grads[:, HEAD:].astype(jnp.bfloat16)
    query_grad = rotate(queries_grad, cosine_table[:, None, :], -sine_table[:, None, :])
    query_grad = query_grad.reshape(tok_rows, HEADS * HEAD).astype(jnp.bfloat16)
    lifted_grad = dot_across(query_norm, query_grad)
    compact_grad = dot_transposed(query_grad, up_query)
    query_value, query_pull = jax.vjp(norm_apply, query_low, gain_query.astype(jnp.float32))
    latent_grad, compact_gain = query_pull(compact_grad)
    latent_grad = latent_grad.astype(jnp.bfloat16)
    compress_grad = dot_across(normed_in, latent_grad)
    keymap_grad = dot_across(normed_in, key_grad)
    valuemap_grad = dot_across(normed_in, value_grad)
    entry_grad = (
        dot_transposed(latent_grad, down_query)
        + dot_transposed(key_grad, key_weights)
        + dot_transposed(value_grad, value_weights)
    )
    first_value, first_pull = jax.vjp(norm_apply, inputs, gain_first.astype(jnp.float32))
    inputs_grad, first_grad = first_pull(entry_grad)
    inputs_grad = inputs_grad + mid_grad
    layer_grads = (
        lax.psum_scatter(first_grad, ("dp", "seq"), scatter_dimension=0, tiled=True),
        lax.psum_scatter(compress_grad, ("dp", "seq"), scatter_dimension=0, tiled=True),
        lax.psum_scatter(compact_gain, ("dp", "seq"), scatter_dimension=0, tiled=True),
        lax.psum_scatter(lifted_grad, ("dp", "seq"), scatter_dimension=0, tiled=True),
        lax.psum_scatter(keymap_grad, ("dp", "seq"), scatter_dimension=0, tiled=True),
        lax.psum_scatter(valuemap_grad, ("dp", "seq"), scatter_dimension=0, tiled=True),
        lax.psum_scatter(output_grad, ("dp", "seq"), scatter_dimension=0, tiled=True),
        lax.psum_scatter(second_grad, ("dp", "seq"), scatter_dimension=0, tiled=True),
    )
    return (
        layer_out[None],
        inputs_grad[None],
        layer_grads[0],
        layer_grads[1],
        layer_grads[2],
        layer_grads[3],
        layer_grads[4],
        layer_grads[5],
        layer_grads[6],
        layer_grads[7],
        feed_grads[0],
        feed_grads[1],
        feed_grads[2],
    )


def tie(*values):
    return lax.optimization_barrier(values)


def gather_rows(block, row_count):
    row_at = lax.axis_index("dp")
    result = jnp.zeros((row_count,) + block.shape, block.dtype)
    result = lax.dynamic_update_index_in_dim(result, block, row_at, 0)
    for hop in range(1, row_count):
        moved = lax.ppermute(block, "dp", [(i, i ^ hop) for i in range(row_count)])
        result = lax.dynamic_update_index_in_dim(result, moved, row_at ^ hop, 0)
    return result


def sum_rows(blocks, row_count):
    row_at = lax.axis_index("dp")
    total = lax.dynamic_index_in_dim(blocks, row_at, 0, False).astype(jnp.float32)
    for hop in range(1, row_count):
        given = lax.dynamic_index_in_dim(blocks, row_at ^ hop, 0, False)
        moved = lax.ppermute(given, "dp", [(i, i ^ hop) for i in range(row_count)])
        total = total + moved.astype(jnp.float32)
    return total


def swap_rows(block, hop):
    return lax.ppermute(block, "dp", [(i, i ^ hop) for i in range(4)])


class SquareSum:
    def __init__(self, product, size, axis, first, second):
        row_at = lax.axis_index("dp")
        self.product, self.axis = product, axis
        self.first, self.second = first, second
        self.half, self.quarter = size // 2, size // 4
        self.upper_half = (row_at // first) % 2
        self.upper_quarter = (row_at // second) % 2

    def make(self, half, quarter):
        return self.product(half * self.half + quarter * self.quarter, self.quarter)

    def give(self, quarter):
        return self.make(1 - self.upper_half, quarter).astype(jnp.bfloat16)

    def give_passed(self):
        return self.give(1 - self.upper_quarter)

    def give_kept(self):
        return self.give(self.upper_quarter)

    def send(self, block):
        return swap_rows(block, self.first)

    def pass_on(self, moved):
        own = self.make(self.upper_half, 1 - self.upper_quarter)
        return swap_rows((own + moved.astype(jnp.float32)).astype(jnp.bfloat16), self.second)

    def finish(self, moved, passed):
        own = self.make(self.upper_half, self.upper_quarter)
        return (own + moved.astype(jnp.float32) + passed.astype(jnp.float32)).astype(
            jnp.bfloat16
        )

    def spread_once(self, own):
        return swap_rows(own, self.first), swap_rows(own, self.second)

    def spread_twice(self, beside):
        return swap_rows(beside, self.first)

    def assemble(self, result, base, own, across, beside, far):
        for block, half, quarter in (
            (own, self.upper_half, self.upper_quarter),
            (beside, self.upper_half, 1 - self.upper_quarter),
            (across, 1 - self.upper_half, self.upper_quarter),
            (far, 1 - self.upper_half, 1 - self.upper_quarter),
        ):
            start = base + half * self.half + quarter * self.quarter
            result = lax.dynamic_update_slice_in_dim(
                result, block.astype(jnp.float32), start, self.axis
            )
        return result


def turn(block, cosine, sine):
    half = block.shape[-1] // 2
    first, second = block[:, :half], block[:, half:]
    return jnp.concatenate([first * cosine - second * sine, second * cosine + first * sine], -1)


def kv_block(kv_ref, at):
    rows = kv_ref.shape[1] // 2
    return jnp.concatenate([kv_ref[at, :rows], kv_ref[at, rows:]], -1)


def low_block(low_ref, gain_ref):
    low = jnp.concatenate([low_ref[i] for i in range(low_ref.shape[0])], -1).astype(jnp.float32)
    gain = jnp.concatenate([gain_ref[i : i + 1] for i in range(gain_ref.shape[0])], -1)
    scale = lax.rsqrt(jnp.mean(low * low, -1, keepdims=True) + epsilon)
    return low * scale, gain


def block_weights(query, kv_ref, seg_query_ref, seg_key_ref, step, parts):
    rows = query.shape[0]
    keys = jnp.concatenate([kv_block(kv_ref, j) for j in range(step + 1)], 0)
    logits = dot_transposed(query, keys) * query.shape[1] ** (-0.5)
    count = (step + 1) * rows
    row_at = step * rows + lax.broadcasted_iota(jnp.int32, (rows, count), 0)
    col_at = lax.broadcasted_iota(jnp.int32, (rows, count), 1)
    allowed = (col_at <= row_at) & (seg_query_ref[...] == seg_key_ref[:, :count])
    logits = jnp.where(allowed, logits, masked_value)
    powers = jnp.exp(logits - jnp.max(logits, -1, keepdims=True))
    return powers / jnp.sum(powers, -1, keepdims=True), keys


def attend_kernel(
    parts,
    low_ref,
    kv_ref,
    gain_ref,
    cosine_ref,
    sine_ref,
    seg_query_ref,
    seg_key_ref,
    up_ref,
    out_ref,
    mixed_ref,
    queries_ref,
    attended_ref,
    norm_ref,
):
    def block(step):
        unit, gain = low_block(low_ref, gain_ref)
        query_norm = (unit * gain).astype(jnp.bfloat16)
        norm_ref[...] = query_norm
        raw = matmul(query_norm, up_ref[...])
        values = jnp.concatenate([kv_block(kv_ref, parts + j) for j in range(step + 1)], 0)
        for head in range(raw.shape[1] // HEAD):
            cols = slice(head * HEAD, (head + 1) * HEAD)
            query = turn(raw[:, cols], cosine_ref[...], sine_ref[...]).astype(jnp.bfloat16)
            queries_ref[:, cols] = query
            weights, _ = block_weights(query, kv_ref, seg_query_ref, seg_key_ref, step, parts)
            attended_ref[:, cols] = matmul(weights.astype(jnp.bfloat16), values).astype(
                jnp.bfloat16
            )
        mixed_ref[...] = matmul(attended_ref[...], out_ref[...]).astype(jnp.bfloat16)

    for step in range(parts):
        pl.when(pl.program_id(0) == step)(functools.partial(block, step))


def attend_back_kernel(
    parts,
    grad_ref,
    queries_ref,
    low_ref,
    kv_ref,
    gain_ref,
    cosine_ref,
    sine_ref,
    seg_query_ref,
    seg_key_ref,
    up_ref,
    out_ref,
    back_ref,
    query_grad_ref,
    keys_sum,
    values_sum,
    means,
):
    slots = low_ref.shape[0]
    lanes = low_ref.shape[2]

    def block(step):
        unit, gain = low_block(low_ref, gain_ref)
        rows = unit.shape[0]
        scale_value = HEAD ** (-0.5)
        context = dot_transposed(grad_ref[...], out_ref[...]).astype(jnp.bfloat16)
        values = jnp.concatenate([kv_block(kv_ref, parts + j) for j in range(step + 1)], 0)
        count = (step + 1) * rows
        last = slice(step * rows, count)
        keys_sum[last] = jnp.zeros((rows, HEAD), jnp.float32)
        values_sum[last] = jnp.zeros((rows, HEAD), jnp.float32)
        for head in range(context.shape[1] // HEAD):
            cols = slice(head * HEAD, (head + 1) * HEAD)
            query = queries_ref[:, cols]
            weights, keys = block_weights(query, kv_ref, seg_query_ref, seg_key_ref, step, parts)
            probs = dot_transposed(context[:, cols], values)
            inner = jnp.sum(weights * probs, -1, keepdims=True)
            logit_grad = (weights * (probs - inner)).astype(jnp.bfloat16)
            turned = matmul(logit_grad, keys) * scale_value
            query_grad_ref[:, cols] = turn(turned, cosine_ref[...], -sine_ref[...]).astype(
                jnp.bfloat16
            )
            keys_sum[:count] += dot_across(logit_grad, query) * scale_value
            values_sum[:count] += dot_across(weights.astype(jnp.bfloat16), context[:, cols])
        compact = dot_transposed(query_grad_ref[...], up_ref[...])
        for slot in range(slots):
            back_ref[slot, last] = compact[:, slot * lanes : (slot + 1) * lanes].astype(
                jnp.bfloat16
            )
        mean = jnp.sum(compact * gain * unit, -1, keepdims=True) / compact.shape[1]
        mean = jnp.broadcast_to(mean, (rows, lanes)).T
        for part in range(rows // lanes):
            at = step * (rows // lanes) + part
            means[at : at + 1] = mean[:1, part * lanes : (part + 1) * lanes]
        if step == parts - 1:
            length = parts * rows
            mean_high = means[...].astype(jnp.bfloat16)
            mean_low = (means[...] - mean_high.astype(jnp.float32)).astype(jnp.bfloat16)
            tail = length + 2 * rows
            size = means.shape[0]
            for slot in range(slots):
                total = keys_sum if slot < parts else values_sum
                own = total[(slot % parts) * rows : (slot % parts + 1) * rows].astype(jnp.bfloat16)
                back_ref[slot, length : length + rows] = own[:, :lanes]
                back_ref[slot, length + rows : tail] = own[:, lanes:]
                back_ref[slot, tail : tail + size] = mean_high
                back_ref[slot, tail + size : tail + 2 * size] = mean_low

    for step in range(parts):
        pl.when(pl.program_id(0) == step)(functools.partial(block, step))


def attention_specs(parts, slots, length, lanes, low_width, head_width, width):
    rows = length // parts
    return [
        pl.BlockSpec((slots, rows, lanes), lambda i: (0, i, 0)),
        pl.BlockSpec((slots, 2 * rows, lanes), lambda i: (0, length // (2 * rows), 0)),
        pl.BlockSpec((slots, lanes), lambda i: (0, 0)),
        pl.BlockSpec((rows, HEAD // 2), lambda i: (i, 0)),
        pl.BlockSpec((rows, HEAD // 2), lambda i: (i, 0)),
        pl.BlockSpec((rows, 1), lambda i: (i, 0)),
        pl.BlockSpec((1, length), lambda i: (0, 0)),
        pl.BlockSpec((low_width, head_width), lambda i: (0, 0)),
        pl.BlockSpec((head_width, width), lambda i: (0, 0)),
    ]


def attend(parts, low_all, gain, cosine, sine, segment_row, up_mine, out_mine):
    slots, _, lanes = low_all.shape
    length = segment_row.shape[0]
    low_width, head_width = up_mine.shape
    width = out_mine.shape[1]
    rows = length // parts
    bf16 = jnp.bfloat16
    return pl.pallas_call(
        functools.partial(attend_kernel, parts),
        grid=(parts,),
        in_specs=attention_specs(parts, slots, length, lanes, low_width, head_width, width),
        out_specs=[
            pl.BlockSpec((rows, width), lambda i: (i, 0)),
            pl.BlockSpec((rows, head_width), lambda i: (i, 0)),
            pl.BlockSpec((rows, head_width), lambda i: (i, 0)),
            pl.BlockSpec((rows, low_width), lambda i: (i, 0)),
        ],
        out_shape=[
            jax.ShapeDtypeStruct((length, width), bf16),
            jax.ShapeDtypeStruct((length, head_width), bf16),
            jax.ShapeDtypeStruct((length, head_width), bf16),
            jax.ShapeDtypeStruct((length, low_width), bf16),
        ],
        compiler_params=pltpu.CompilerParams(vmem_limit_bytes=48 * 1024 * 1024),
        cost_estimate=pl.CostEstimate(
            flops=8 * 10**9, bytes_accessed=16 * 10**6, transcendentals=2 * 10**6
        ),
        name="attend",
    )(
        low_all,
        low_all,
        gain,
        cosine,
        sine,
        segment_row[:, None],
        segment_row[None],
        up_mine,
        out_mine,
    )


def attend_back(
    parts, grad, queries, low_all, gain, cosine, sine, segment_row, up_mine, out_mine
):
    slots, _, lanes = low_all.shape
    length = segment_row.shape[0]
    low_width, head_width = up_mine.shape
    width = out_mine.shape[1]
    rows = length // parts
    means = length // lanes
    total = length + 2 * rows + 2 * means
    bf16 = jnp.bfloat16
    return pl.pallas_call(
        functools.partial(attend_back_kernel, parts),
        grid=(parts,),
        in_specs=[
            pl.BlockSpec((rows, width), lambda i: (i, 0)),
            pl.BlockSpec((rows, head_width), lambda i: (i, 0)),
        ]
        + attention_specs(parts, slots, length, lanes, low_width, head_width, width),
        out_specs=[
            pl.BlockSpec((slots, total, lanes), lambda i: (0, 0, 0)),
            pl.BlockSpec((rows, head_width), lambda i: (i, 0)),
        ],
        out_shape=[
            jax.ShapeDtypeStruct((slots, total, lanes), bf16),
            jax.ShapeDtypeStruct((length, head_width), bf16),
        ],
        scratch_shapes=[
            pltpu.VMEM((length, HEAD), jnp.float32),
            pltpu.VMEM((length, HEAD), jnp.float32),
            pltpu.VMEM((means, lanes), jnp.float32),
        ],
        compiler_params=pltpu.CompilerParams(vmem_limit_bytes=48 * 1024 * 1024),
        cost_estimate=pl.CostEstimate(
            flops=12 * 10**9, bytes_accessed=20 * 10**6, transcendentals=2 * 10**6
        ),
        name="attend_back",
    )(
        grad,
        queries,
        low_all,
        low_all,
        gain,
        cosine,
        sine,
        segment_row[:, None],
        segment_row[None],
        up_mine,
        out_mine,
    )


def local_heads(
    row_count,
    seq_count,
    layer_input,
    segment_ids,
    first_gain,
    query_down,
    query_gain,
    query_up,
    key_proj,
    value_proj,
    out_proj,
    second_gain,
    w_gate,
    w_up,
    w_down,
    cotangent,
):
    f32, bf16 = jnp.float32, jnp.bfloat16
    seq_at = lax.axis_index("seq")
    core_at = lax.rem(seq_at, 2)
    swap = [(i, i ^ 1) for i in range(seq_count)]
    own_rows = layer_input.shape[1]
    length = own_rows * seq_count
    width = layer_input.shape[2]
    low_width = query_down.shape[1]
    down_rows = query_down.shape[0]
    up_rows = query_up.shape[0]
    out_rows = out_proj.shape[0]
    half_count = row_count // 2
    chips = seq_count // 2
    own_low = low_width // seq_count
    low_part = own_low // row_count
    kv_parts = seq_count // 2
    kv_rows = length // kv_parts
    kv_at = lax.rem(seq_at, kv_parts)
    is_key = seq_at < kv_parts
    spare = 8
    own_heads = half_count

    gains = jnp.zeros((spare, own_low + HEAD), bf16)
    gains = gains.at[0, :down_rows].set(first_gain)
    gains = gains.at[1, :down_rows].set(second_gain)
    gains = gains.at[2, :up_rows].set(query_gain)
    low_cols = query_down.reshape(down_rows, row_count, seq_count, low_part)
    low_cols = low_cols.transpose(2, 0, 1, 3).reshape(seq_count, down_rows, own_low)
    kv_cols = jnp.stack([key_proj] * kv_parts + [value_proj] * kv_parts)
    sent = jnp.concatenate([low_cols, kv_cols], -1)
    sent = jnp.concatenate(
        [sent, jnp.broadcast_to(gains[None], (seq_count, spare, own_low + HEAD))], 1
    )
    sent = sent.reshape(seq_count * (down_rows + spare), own_low + HEAD)
    sent = lax.all_to_all(sent, "seq", 0, 0, tiled=True)
    entry_all = gather_rows(sent, row_count)
    entry_all = entry_all.reshape(row_count * seq_count, down_rows + spare, own_low + HEAD)
    entry_weights = entry_all[:, :down_rows].reshape(width, own_low + HEAD)
    gain_first = entry_all[:, down_rows, :down_rows].reshape(width).astype(f32)
    gain_second = entry_all[:, down_rows + 1, :down_rows].reshape(width).astype(f32)
    gain_query = entry_all[:, down_rows + 2, :up_rows].reshape(row_count, seq_count, low_part)
    gain_query = gain_query.transpose(1, 0, 2).reshape(low_width).astype(f32)

    inputs_all = lax.all_gather(layer_input[0], "seq", axis=0, tiled=True)

    up_sent = query_up.reshape(up_rows, 2, half_count, chips, HEAD).transpose(3, 1, 0, 2, 4)
    up_sent = up_sent.reshape(seq_count * up_rows, own_heads * HEAD)
    up_mine = lax.all_to_all(up_sent, "seq", 0, 0, tiled=True)
    up_mine = gather_rows(up_mine, row_count)
    up_mine = up_mine.reshape(row_count, seq_count, low_part, own_heads * HEAD)
    up_mine = up_mine.transpose(1, 0, 2, 3).reshape(low_width, own_heads * HEAD)

    out_all = gather_rows(out_proj, row_count)
    out_kept = lax.dynamic_slice_in_dim(out_all, core_at * half_count, half_count, 0)
    out_given = lax.dynamic_slice_in_dim(out_all, (1 - core_at) * half_count, half_count, 0)
    out_got = lax.ppermute(out_given, "seq", swap)
    out_mine = jnp.where(
        core_at == 0,
        jnp.stack([out_kept, out_got], 1),
        jnp.stack([out_got, out_kept], 1),
    ).reshape(own_heads * HEAD, width)

    cot_rows = cotangent[0]
    cot_all = lax.all_gather(cot_rows, "seq", axis=0, tiled=True)

    positions = jnp.arange(length, dtype=jnp.int32)
    cosine_table, sine_table = angle_tables(positions, HEAD)

    inputs_wide = inputs_all.astype(f32)
    entry_scale = lax.rsqrt(jnp.mean(inputs_wide * inputs_wide, -1, keepdims=True) + epsilon)
    normed_in = (inputs_wide * entry_scale * gain_first).astype(bf16)
    low_own = matmul(normed_in, entry_weights)
    kv_own = lax.dynamic_slice_in_dim(low_own[:, own_low:], kv_at * kv_rows, kv_rows, 0)
    kv_cos = lax.dynamic_slice_in_dim(cosine_table, kv_at * kv_rows, kv_rows, 0)
    kv_sin = lax.dynamic_slice_in_dim(sine_table, kv_at * kv_rows, kv_rows, 0)
    kv_own = jnp.where(is_key, rotate(kv_own, kv_cos, kv_sin), kv_own).astype(bf16)
    half_head = HEAD // 2
    low_sent = jnp.concatenate(
        [low_own[:, :own_low].astype(bf16), kv_own[:, :half_head], kv_own[:, half_head:]], 0
    )
    low_all = lax.all_gather(low_sent, "seq", axis=0, tiled=False)

    segment_row = segment_ids[0]
    gain_slots = gain_query.reshape(seq_count, own_low)
    half_cos, half_sin = cosine_table[:, :half_head], sine_table[:, :half_head]
    mixed, queries, attended, query_norm = attend(
        kv_parts, low_all, gain_slots, half_cos, half_sin, segment_row, up_mine, out_mine
    )
    mixed = lax.psum_scatter(mixed, "seq", scatter_dimension=0, tiled=True).astype(f32)
    mid_sum = layer_input[0].astype(f32) + mixed
    mid_scale = lax.rsqrt(jnp.mean(mid_sum * mid_sum, -1, keepdims=True) + epsilon)
    mid_unit = mid_sum * mid_scale
    normed_mid = (mid_unit * gain_second).astype(bf16)

    grad_hidden = dot_transposed(cot_all, w_down)
    normed_mid, grad_hidden = tie(normed_mid, grad_hidden)
    normed_all = lax.all_gather(normed_mid, "seq", axis=0, tiled=True)
    gate_pre = matmul(normed_all, w_gate)
    up_pre = matmul(normed_all, w_up)
    hidden = gated_unit(gate_pre, up_pre)
    gated_value, gate_pull = jax.vjp(gated_unit, gate_pre, up_pre)
    hidden = gated_value.astype(bf16)
    gate_grad, up_grad = gate_pull(grad_hidden)
    gate_grad = gate_grad.astype(bf16)
    up_grad = up_grad.astype(bf16)
    normed_grad = dot_transposed(gate_grad, w_gate) + dot_transposed(up_grad, w_up)
    normed_grad = lax.psum_scatter(
        normed_grad.astype(bf16), "seq", scatter_dimension=0, tiled=True
    ).astype(f32)
    def from_columns(left, right):
        return lambda start, size: dot_across(
            lax.dynamic_slice_in_dim(left, start, size, 1), right
        )

    def to_columns(left, right, base):
        return lambda start, size: dot_across(
            left, lax.dynamic_slice_in_dim(right, base + start, size, 1)
        )

    half_width = width // 2
    sums = [
        SquareSum(from_columns(normed_all, gate_grad), width, 0, 1, 2),
        SquareSum(from_columns(normed_all, up_grad), width, 0, 2, 1),
        SquareSum(to_columns(hidden, cot_all, 0), half_width, 1, 1, 2),
        SquareSum(to_columns(hidden, cot_all, half_width), half_width, 1, 2, 1),
    ]
    passed = [one.send(one.give_passed()) for one in sums]
    moved = [one.send(one.give_kept()) for one in sums]
    hidden_out = matmul(hidden, w_down).astype(bf16)
    normed_grad, hidden_out, moved, passed = tie(normed_grad, hidden_out, moved, passed)
    passed = [one.pass_on(block) for one, block in zip(sums, passed)]
    owned = [one.finish(block, more) for one, block, more in zip(sums, moved, passed)]

    second_grad = jnp.sum(normed_grad * mid_unit, 0)
    scaled_grad = normed_grad * gain_second
    mid_grad = mid_scale * (
        scaled_grad - mid_unit * jnp.mean(scaled_grad * mid_unit, -1, keepdims=True)
    )
    mid_grad = mid_grad + cot_rows.astype(f32)
    attn_grad = lax.all_gather(mid_grad.astype(bf16), "seq", axis=0, tiled=True)

    attn_grad, owned, hidden_out = tie(attn_grad, owned, hidden_out)
    branch_out = lax.psum_scatter(hidden_out, "seq", scatter_dimension=0, tiled=True)
    back_sent, query_grad = attend_back(
        kv_parts,
        attn_grad,
        queries,
        low_all,
        gain_slots,
        half_cos,
        half_sin,
        segment_row,
        up_mine,
        out_mine,
    )
    output_grad = dot_across(attended, attn_grad).astype(bf16)
    output_grad = output_grad.reshape(own_heads, 2, out_rows, width)
    grad_kept = lax.dynamic_index_in_dim(output_grad, core_at, 1, False)
    grad_given = lax.dynamic_index_in_dim(output_grad, 1 - core_at, 1, False)
    grad_got = lax.ppermute(grad_given, "seq", swap)
    output_grad = jnp.where(
        core_at == 0,
        jnp.concatenate([grad_kept, grad_got], 0),
        jnp.concatenate([grad_got, grad_kept], 0),
    )
    output_grad = sum_rows(output_grad, row_count)
    spread = [one.spread_once(block) for one, block in zip(sums[2:], owned[2:])]
    back_sent, branch_out, output_grad, owned[0], owned[1], spread = tie(
        back_sent, branch_out, output_grad, owned[0], owned[1], spread
    )
    spread = [one.spread_once(block) for one, block in zip(sums[:2], owned[:2])] + spread
    back = lax.psum_scatter(back_sent, "seq", scatter_dimension=0, tiled=False).astype(f32)

    lifted_grad = dot_across(query_norm, query_grad).astype(bf16)
    lifted_grad = lifted_grad.reshape(seq_count, row_count, up_rows, own_heads * HEAD)
    lifted_grad = lifted_grad.transpose(1, 0, 2, 3)
    lifted_grad = lifted_grad.reshape(row_count, seq_count * up_rows, own_heads * HEAD)
    lifted_grad = sum_rows(lifted_grad, row_count).astype(bf16)
    back, lifted_grad, spread = tie(back, lifted_grad, spread)

    compact_own = back[:length]
    kv_back = jnp.concatenate(
        [back[length : length + kv_rows], back[length + kv_rows : length + 2 * kv_rows]], -1
    )
    mean_back = back[length + 2 * kv_rows :].reshape(2, length).sum(0)[:, None]
    low_at = seq_at * own_low
    query_low = low_all[:, :length].astype(f32)
    query_scale = jnp.sum(query_low * query_low, (0, 2)) / low_width
    query_scale = lax.rsqrt(query_scale + epsilon)[:, None]
    low_mine = lax.dynamic_index_in_dim(low_all, seq_at, 0, False)[:length].astype(f32)
    unit_own = low_mine * query_scale
    gain_own = lax.dynamic_slice_in_dim(gain_query, low_at, own_low, 0)
    compact_gain = jnp.sum(compact_own * unit_own, 0)
    latent_grad = (query_scale * (compact_own * gain_own - unit_own * mean_back)).astype(bf16)
    kv_back = jnp.where(is_key, rotate(kv_back, kv_cos, -kv_sin), kv_back).astype(bf16)
    kv_padded = lax.dynamic_update_slice_in_dim(
        jnp.zeros((length, HEAD), bf16), kv_back, kv_at * kv_rows, 0
    )
    entry_sent = jnp.concatenate([latent_grad, kv_padded], -1)
    entry_part = dot_transposed(entry_sent, entry_weights)
    blocks_of = [
        (own, across, beside, one.spread_twice(beside))
        for one, own, (across, beside) in zip(sums, owned, spread)
    ]
    units = w_gate.shape[1]
    gating_grad = sums[0].assemble(jnp.zeros((width, units), f32), 0, *blocks_of[0])
    upward_grad = sums[1].assemble(jnp.zeros((width, units), f32), 0, *blocks_of[1])
    down_grad = sums[2].assemble(jnp.zeros((units, width), f32), 0, *blocks_of[2])
    down_grad = sums[3].assemble(down_grad, half_width, *blocks_of[3])
    entry_grad = lax.psum_scatter(
        entry_part.astype(bf16), "seq", scatter_dimension=0, tiled=True
    ).astype(f32)
    first_grad = jnp.sum(entry_part * (inputs_wide * entry_scale), 0)
    blocks = row_count * seq_count
    weight_grad = dot_across(normed_in, entry_sent).astype(bf16)
    weight_grad = weight_grad.reshape(blocks, down_rows, own_low + HEAD)
    mine = (jnp.arange(seq_count) == seq_at)[None, :, None]
    gain_back = jnp.where(mine, compact_gain.reshape(row_count, 1, low_part), 0.0)
    extra = jnp.zeros((blocks, spare, own_low + HEAD), f32)
    extra = extra.at[:, 0, :down_rows].set(first_grad.reshape(blocks, down_rows))
    extra = extra.at[:, 1, :down_rows].set(second_grad.reshape(blocks, down_rows))
    extra = extra.at[:, 2, :low_part].set(gain_back.reshape(blocks, low_part))
    weight_grad = jnp.concatenate([weight_grad, extra.astype(bf16)], 1)
    weight_grad = weight_grad.reshape(
        row_count, seq_count * (down_rows + spare), own_low + HEAD
    )
    lifted_grad = lax.all_to_all(lifted_grad, "seq", 0, 0, tiled=True)
    lifted_grad = lifted_grad.reshape(chips, 2, up_rows, half_count, HEAD)
    lifted_grad = lifted_grad.transpose(2, 1, 3, 0, 4).reshape(up_rows, HEADS * HEAD)
    weight_grad = sum_rows(weight_grad, row_count).astype(bf16)
    weight_grad, lifted_grad = tie(weight_grad, lifted_grad)
    weight_grad = lax.all_to_all(weight_grad, "seq", 0, 0, tiled=True).astype(f32)
    weight_grad = weight_grad.reshape(seq_count, down_rows + spare, own_low + HEAD)
    compress_grad = weight_grad[:, :down_rows, :own_low].reshape(
        seq_count, down_rows, row_count, low_part
    )
    compress_grad = compress_grad.transpose(1, 2, 0, 3).reshape(down_rows, low_width)
    keymap_grad = jnp.sum(weight_grad[:kv_parts, :down_rows, own_low:], 0)
    valuemap_grad = jnp.sum(weight_grad[kv_parts:, :down_rows, own_low:], 0)
    gain_rows = jnp.sum(weight_grad[:, down_rows:], 0)
    entry_grad, compress_grad, lifted_grad, output_grad, spread = tie(
        entry_grad, compress_grad, lifted_grad, output_grad, spread
    )
    layer_out = mid_sum + branch_out.astype(f32)
    own_at = seq_at * own_rows
    inputs_own = layer_input[0].astype(f32)
    scale_own = lax.dynamic_slice_in_dim(entry_scale, own_at, own_rows, 0)
    entry_unit = inputs_own * scale_own
    entry_scaled = entry_grad * gain_first
    inputs_grad = scale_own * (
        entry_scaled - entry_unit * jnp.mean(entry_scaled * entry_unit, -1, keepdims=True)
    )
    inputs_grad = inputs_grad + mid_grad

    return (
        layer_out[None],
        inputs_grad[None],
        gain_rows[0, :down_rows],
        compress_grad,
        gain_rows[2, :low_part],
        lifted_grad.astype(f32),
        keymap_grad,
        valuemap_grad,
        output_grad.astype(f32),
        gain_rows[1, :down_rows],
        gating_grad,
        upward_grad,
        down_grad,
    )


def solution(mesh):
    row_count, seq_count = mesh.shape["dp"], mesh.shape["seq"]
    if row_count == 4 and seq_count % 2 == 0 and HEADS * 2 == row_count * seq_count:
        local = functools.partial(local_heads, row_count, seq_count)
    else:
        local = local_tokens
    return jax.shard_map(
        local,
        mesh=mesh,
        in_specs=(
            P("dp", "seq", None),
            P("dp", None),
            P(("dp", "seq")),
            P(("dp", "seq"), None),
            P(("dp", "seq")),
            P(("dp", "seq"), None),
            P(("dp", "seq"), None),
            P(("dp", "seq"), None),
            P(("dp", "seq"), None),
            P(("dp", "seq")),
            P(None, "seq"),
            P(None, "seq"),
            P("seq", None),
            P("dp", "seq", None),
        ),
        out_specs=(
            P("dp", "seq", None),
            P("dp", "seq", None),
            P(("dp", "seq")),
            P(("dp", "seq"), None),
            P(("dp", "seq")),
            P(("dp", "seq"), None),
            P(("dp", "seq"), None),
            P(("dp", "seq"), None),
            P(("dp", "seq"), None),
            P(("dp", "seq")),
            P(None, "seq"),
            P(None, "seq"),
            P("seq", None),
        ),
        check_vma=False,
    )
```
